32 devices in a mesh: dp: 8 (over y, x, core), seq: 4 (over z).
Axes of the slice: x: 2, y: 2, z: 4, core: 2. Of those that a mesh axis runs over, the one named last changes fastest.
Arguments:
- cotangent: bfloat16 [8, 512, 2048], P('dp', 'seq'), may hold values from -1.75 to 1.75
- expert_ids: int32 [8, 512, 2], P('dp', 'seq'), may hold values from 0 to 15, as said below
- gate_probs: float32 [8, 512, 2], P('dp', 'seq'), may hold values from 0.05 to 1
- hidden_acts: bfloat16 [7168, 512], P('seq', 'dp'), may hold values from -6 to 6
- step_input: bfloat16 [8, 512, 256], P('dp', 'seq'), may hold values from -6 to 6
- step_proj: bfloat16 [256, 4096], replicated, may hold values from -0.375 to 0.375
- step_bias: float32 [4096], replicated, may hold values from -1 to 1
- decay_rate: float32 [16, 4096], replicated, may hold values from 0.0009765625 to 0.05
- input_coef: float32 [8, 16, 512], P('dp', None, 'seq'), may hold values from -4 to 4
- output_coef: float32 [8, 16, 512], P('dp', None, 'seq'), may hold values from -0.625 to 0.625
- grad_output: bfloat16 [8, 512, 4096], P('dp', 'seq'), may hold values from -6 to 6
- skip_weight: float32 [4096], replicated, may hold values from 0.5 to 1.5
Outputs:
- grad_down: float32 [2048, 7168], P('dp', 'seq')
- grad_x: bfloat16 [8, 512, 4096], P('dp', 'seq')
The draws below stay inside these ranges and needn't reach their ends.
Inputs may be any that keep to these rules, and one draw needn't show every extreme that they name: `expert_ids`: each token names 2 different experts; among the tokens of one device (aligned blocks of 128 tokens of a sequence) every expert is named by exactly 16 of the pairs.
All inputs are finite; a program needn't handle non-finite values.
Results may differ from the reference program's by a relative error of at most 0.0029.
Values may be sent and summed in bfloat16 or wider, within the bound.
No kernel may reach another device: no remote copies, remote signals or barrier semaphores. Data moves between devices by JAX's collectives and lax.ppermute only.
A program may use at most 64 MiB of HBM per device.

```python
import math
import jax
import jax.numpy as jnp
from jax import lax

D = 2048
TOP = 2
EXPERTS = 16
HIDDEN_SIZE = 7168
CH = 4096
STATE = 16
DT_RANK = 256
TOK_DEV = 128
CAP = 16
ROWS = 64
LENGTH = 512
SEQS = 8
N_SEQ = 4


def draw_expert_ids(key, part):
    block_count = SEQS * (LENGTH // TOK_DEV)
    per_group = TOK_DEV // EXPERTS

    def one_block(position):
        token_key = jax.random.fold_in(key, 2 * position)
        cycle_key = jax.random.fold_in(key, 2 * position + 1)
        shuffled = jax.random.permutation(token_key, TOK_DEV)
        primary = jnp.zeros((TOK_DEV,), jnp.int32).at[shuffled].set(jnp.arange(TOK_DEV, dtype=jnp.int32) // per_group)
        labels = jax.random.permutation(cycle_key, EXPERTS).astype(jnp.int32)
        successor = jnp.zeros((EXPERTS,), jnp.int32).at[labels].set(jnp.roll(labels, -1))
        secondary = successor[primary]
        return jnp.stack([primary, secondary], axis=-1)
    blocks = jax.vmap(one_block)(jnp.arange(block_count, dtype=jnp.int32))
    return blocks.reshape(SEQS, LENGTH, TOP).astype(jnp.int32)


def strengthened(drawn, own_key, source, target, shards_of, factor):
    owner, partner = [(jnp.arange(drawn.shape[dim]) // (drawn.shape[dim] // shards_of)).reshape([-1 if axis == dim else 1 for axis in range(drawn.ndim)]) for dim in (source, target)]
    chosen = jax.random.permutation(own_key, shards_of)[partner]
    strong = (owner == chosen) | (owner == (partner + shards_of // 2) % shards_of)
    return jnp.where(strong, factor * drawn, drawn)


def block_scale(key, shape, split, least, high):
    level = 1.0
    for axis_at, blocks in split:
        draws = jax.random.uniform(jax.random.fold_in(jax.random.fold_in(key, 6), axis_at), (blocks,), jnp.float32, least / len(split), high / len(split))
        level = level * jnp.repeat(jnp.exp(draws), shape[axis_at] // blocks).reshape((-1,) + (1,) * (len(shape) - 1 - axis_at))
    return level


def normal_values(key, shape, scale, bound, split=(), held_as=jnp.bfloat16):
    array = scale * jax.random.normal(key, shape, jnp.float32)
    if split:
        array = array * block_scale(key, shape, split, -0.22, 0.18)
    return jnp.clip(array, -bound, bound).astype(held_as)


def heavy_noise(key, dims, scale, limit, cuts, heavy, kind=jnp.bfloat16):
    drawn = scale * jax.random.normal(key, dims, jnp.float32)
    if cuts:
        drawn = drawn * block_scale(key, dims, cuts, -0.22, 0.18)
    return jnp.clip(strengthened(drawn, jax.random.fold_in(key, 3), *heavy), -limit, limit).astype(kind)


def setup_inputs(seed: int = 0) -> dict:
    keys = jax.random.split(jax.random.key(seed), 13)
    return {
        "cotangent": heavy_noise(keys[0], (SEQS, LENGTH, D), (2.0 / (SEQS * ROWS) ** 0.5), 1.75, ((0, 8), (1, 4)), (0, 2, 8, 2.0)),
        "expert_ids": draw_expert_ids(jax.random.fold_in(keys[12], 71), 0),
        "gate_probs": jnp.clip(0.05 + 0.95 * jax.random.uniform(keys[2], (SEQS, LENGTH, TOP), jnp.float32) ** block_scale(keys[2], (SEQS, LENGTH, TOP), ((0, 8), (1, 4)), -0.2, 0.2), 0.05, 1.0),
        "hidden_acts": normal_values(keys[3], (HIDDEN_SIZE, SEQS * ROWS), 1.0, 6.0, ((0, 4), (1, 8))),
        "step_input": normal_values(keys[4], (SEQS, LENGTH, DT_RANK), 1.0, 6.0, ((0, 8), (1, 4))),
        "step_proj": normal_values(keys[5], (DT_RANK, CH), DT_RANK ** -0.5, 0.375),
        "step_bias": jnp.clip(jax.random.uniform(keys[6], (CH,), jnp.float32, -1.0, 1.0), -1.0, 1.0),
        "decay_rate": jnp.clip(jnp.exp(jax.random.uniform(keys[7], (STATE, CH), jnp.float32, math.log(0.0009765625), math.log(0.05))), 0.0009765625, 0.05),
        "input_coef": normal_values(keys[8], (SEQS, STATE, LENGTH), 0.25, 4.0, ((0, 8), (2, 4)), jnp.float32),
        "output_coef": normal_values(keys[9], (SEQS, STATE, LENGTH), (1.0 / LENGTH ** 0.5), 0.625, ((0, 8), (2, 4)), jnp.float32),
        "grad_output": normal_values(keys[10], (SEQS, LENGTH, CH), 1.0, 6.0, ((0, 8), (1, 4))),
        "skip_weight": jnp.clip(jax.random.uniform(keys[11], (CH,), jnp.float32, 0.5, 1.5), 0.5, 1.5),
    }


def reference(cotangent, expert_ids, gate_probs, hidden_acts, step_input, step_proj, step_bias, decay_rate, input_coef, output_coef, grad_output, skip_weight):
    pair_count = TOK_DEV * TOP
    block_total = SEQS * N_SEQ
    chosen = (expert_ids.reshape(block_total, pair_count) == 0).astype(jnp.int32)
    before = jnp.cumsum(chosen, axis=1) - chosen
    destination = jnp.where(chosen == 1, before, CAP).astype(jnp.int32)
    block_index = jnp.broadcast_to(jnp.arange(block_total, dtype=jnp.int32)[:, None], (block_total, pair_count))
    pair_token = jnp.broadcast_to((jnp.arange(pair_count, dtype=jnp.int32) // TOP)[None, :], (block_total, pair_count))
    token_of_slot = jnp.zeros((block_total, CAP + 1), jnp.int32).at[block_index, destination].set(pair_token)[:, :CAP]
    gate_of_slot = jnp.zeros((block_total, CAP + 1), gate_probs.dtype).at[block_index, destination].set(gate_probs.reshape(block_total, pair_count))[:, :CAP]
    cot_blocks = cotangent.reshape(block_total, TOK_DEV, D)
    picked = jnp.take_along_axis(cot_blocks, token_of_slot[:, :, None], axis=1)
    routed = (picked.astype(jnp.float32) * gate_of_slot[:, :, None]).astype(jnp.bfloat16).reshape(SEQS * ROWS, D)
    grad_down = jnp.transpose(jnp.dot(hidden_acts.astype(jnp.float32), routed.astype(jnp.float32), precision=lax.Precision.HIGHEST, preferred_element_type=jnp.float32))

    negative_rate = -decay_rate
    proj_wide = step_proj.astype(jnp.float32)

    def token_step(state_carry, inputs):
        step_rows, grad_rows, in_cols, out_cols = inputs
        step_size = jax.nn.softplus(jnp.dot(step_rows.astype(jnp.float32), proj_wide, precision=lax.Precision.HIGHEST, preferred_element_type=jnp.float32) + step_bias[None, :])
        out_grad = grad_rows.astype(jnp.float32)
        adjoint = out_cols[:, :, None] * out_grad[:, None, :] + state_carry
        result = step_size * jnp.sum(in_cols[:, :, None] * adjoint, axis=1) + skip_weight[None, :] * out_grad
        passed = jnp.exp(step_size[:, None, :] * negative_rate[None, :, :]) * adjoint
        return passed, result.astype(jnp.bfloat16)

    inputs = (jnp.moveaxis(step_input, 1, 0), jnp.moveaxis(grad_output, 1, 0), jnp.moveaxis(input_coef, 2, 0), jnp.moveaxis(output_coef, 2, 0))
    final_state, token_rows = lax.scan(token_step, jnp.zeros((SEQS, STATE, CH), jnp.float32), inputs, reverse=True)
    grad_x = jnp.moveaxis(token_rows, 0, 1)
    return (grad_down, grad_x)
```

```python
import functools
import math

import jax
import jax.numpy as jnp
from jax import lax
from jax.experimental import pallas as pl
from jax.experimental.pallas import tpu as pltpu
from jax.sharding import PartitionSpec as P

LANES=128
BLOCK=16
CT=512
VMEM_BYTES=40*2**20
LOG2E=math.log2(math.e)
f32=jnp.float32; bf16=jnp.bfloat16
def softplus(v):
    return jnp.maximum(v,0.0)+jnp.log1p(jnp.exp(-jnp.abs(v)))

def spread(src_ref, dst_ref):
    v=src_ref[...]
    for t in range(v.shape[1]):
        dst_ref[t]=jnp.broadcast_to(v[:,t:t+1],(v.shape[0],LANES))

def state_kernel(x_ref,proj_ref,bias_ref,decay_ref,outc_ref,g_ref,step_ref,msg_ref,outb,g32,stot):
    ct=pl.program_id(0)
    toks=x_ref.shape[0]; n=decay_ref.shape[0]; chunk=decay_ref.shape[1]
    chans=chunk*pl.num_programs(0)
    @pl.when(ct==0)
    def _():
        spread(outc_ref,outb)
    step=softplus(jnp.dot(x_ref[...],proj_ref[...],preferred_element_type=f32)+bias_ref[...])
    blocks=toks//BLOCK
    step_ref[...]=step.reshape(blocks,BLOCK,chunk)
    g32[...]=g_ref[...].astype(f32).reshape(blocks,BLOCK,chunk)
    total=jnp.sum(step,axis=0,keepdims=True)
    width=stot.shape[1]
    for k in range(chunk//width):
        stot[pl.ds(ct*(chunk//width)+k,1),:]=total[:,k*width:(k+1)*width]
    tiles=chunk//LANES
    rate=[decay_ref[:,q*LANES:(q+1)*LANES]*(-LOG2E) for q in range(tiles)]
    def body(b,states):
        b=blocks-1-b
        states=list(states)
        for k in reversed(range(BLOCK)):
            ob=outb[b*BLOCK+k]
            for q in range(tiles):
                sl=pl.ds(q*LANES,LANES)
                s=jnp.broadcast_to(step_ref[b,k:k+1,sl],(n,LANES))
                g=jnp.broadcast_to(g32[b,k:k+1,sl],(n,LANES))
                adj=states[q]+ob*g
                states[q]=jnp.exp2(s*rate[q])*adj
        return tuple(states)
    states=lax.fori_loop(0,toks//BLOCK,body,tuple(jnp.zeros((n,LANES),f32) for _ in range(tiles)))
    for q in range(tiles):
        msg_ref[:,pl.ds(pl.multiple_of(ct*chunk+q*LANES,LANES),LANES)]=states[q].astype(bf16)
    @pl.when(ct==pl.num_programs(0)-1)
    def _():
        s=stot[...]
        hi=s.astype(bf16)
        msg_ref[:,chans:chans+width]=hi
        msg_ref[:,chans+width:chans+2*width]=(s-hi.astype(f32)).astype(bf16)

def state_pass(x,proj,bias,decay,outc,g):
    toks,chans=g.shape; n=decay.shape[0]; width=chans//n
    return pl.pallas_call(state_kernel,grid=(chans//CT,),
        in_specs=[pl.BlockSpec(x.shape,lambda c:(0,0)),pl.BlockSpec((proj.shape[0],CT),lambda c:(0,c)),pl.BlockSpec((1,CT),lambda c:(0,c)),
                  pl.BlockSpec((n,CT),lambda c:(0,c)),pl.BlockSpec(outc.shape,lambda c:(0,0)),pl.BlockSpec((toks,CT),lambda c:(0,c))],
        out_specs=[pl.BlockSpec((toks//BLOCK,BLOCK,CT),lambda c:(0,0,c)),pl.BlockSpec((n,chans+2*width),lambda c:(0,0))],
        out_shape=[jax.ShapeDtypeStruct((toks//BLOCK,BLOCK,chans),f32),jax.ShapeDtypeStruct((n,chans+2*width),bf16)],
        scratch_shapes=[pltpu.VMEM((toks,n,LANES),f32),pltpu.VMEM((toks//BLOCK,BLOCK,CT),f32),pltpu.VMEM((n,width),f32)],
        compiler_params=pltpu.CompilerParams(vmem_limit_bytes=VMEM_BYTES),
        name="state_pass")(x,proj,bias.reshape(1,-1),decay,outc,g)


def full_kernel(step_ref,g_ref,decay_ref,outc_ref,inc_ref,skip_ref,*rest):
    *msgs,out_ref,outb,g32,picks,adjs,stots=rest
    ct=pl.program_id(0)
    toks,chunk=g_ref.shape; n=decay_ref.shape[0]
    chans=chunk*pl.num_programs(0); width=chans//n
    span=BLOCK*n
    blocks=toks//BLOCK
    @pl.when(ct==0)
    def _():
        spread(outc_ref,outb)
        sel=(lax.broadcasted_iota(jnp.int32,(n,span),1)%n==lax.broadcasted_iota(jnp.int32,(n,span),0)).astype(bf16)
        own=(lax.broadcasted_iota(jnp.int32,(toks,span),1)//n==lax.broadcasted_iota(jnp.int32,(toks,span),0)%BLOCK)
        v=inc_ref[...]
        hi=v.astype(bf16); lo=(v-hi.astype(f32)).astype(bf16)
        for part,vals in enumerate((hi,lo)):
            wide=lax.dot_general(vals,sel,(((0,),(0,)),((),())),preferred_element_type=f32)
            wide=jnp.where(own,wide,0.0).astype(bf16)
            for b in range(blocks):
                picks[b,part*BLOCK:(part+1)*BLOCK,:]=wide[b*BLOCK:(b+1)*BLOCK]
        for k,m in enumerate(msgs):
            total=m[:,chans:chans+width].astype(f32)+m[:,chans+width:chans+2*width].astype(f32)
            for row in range(n):
                stots[k,row]=total[row:row+1]
    g32[...]=g_ref[...].astype(f32).reshape(blocks,BLOCK,chunk)
    tiles=chunk//LANES
    rate=[decay_ref[:,q*LANES:(q+1)*LANES]*(-LOG2E) for q in range(tiles)]
    states=[]
    for q in range(tiles):
        lanes=pl.ds(pl.multiple_of(ct*chunk+q*LANES,LANES),LANES)
        acc=msgs[-1][:,lanes].astype(f32)
        for k in reversed(range(len(msgs)-1)):
            tot=stots[k,ct*(chunk//width)+q*LANES//width,:,(q*LANES)%width:(q*LANES)%width+LANES]
            acc=msgs[k][:,lanes].astype(f32)+jnp.exp2(jnp.broadcast_to(tot,(n,LANES))*rate[q])*acc
        states.append(acc)
    def body(i,states):
        b=blocks-1-i
        base=b*BLOCK
        states=list(states)
        for k in reversed(range(BLOCK)):
            ob=outb[base+k]
            for q in range(tiles):
                sl=pl.ds(q*LANES,LANES)
                s=jnp.broadcast_to(step_ref[b,k:k+1,sl],(n,LANES))
                g=jnp.broadcast_to(g32[b,k:k+1,sl],(n,LANES))
                adj=states[q]+ob*g
                adjs[k*n:(k+1)*n,q*LANES:(q+1)*LANES]=adj.astype(bf16)
                states[q]=jnp.exp2(s*rate[q])*adj
        both=jnp.dot(picks[b],adjs[...],preferred_element_type=f32)
        y=both[:BLOCK]+both[BLOCK:]
        rows=pl.ds(pl.multiple_of(base,BLOCK),BLOCK)
        out_ref[rows,:]=(step_ref[b]*y+skip_ref[...]*g32[b]).astype(bf16)
        return tuple(states)
    lax.fori_loop(0,blocks,body,tuple(states))

def full_pass(step,g,decay,outc,inc,skip,msgs):
    toks,chans=g.shape; n=decay.shape[0]; width=chans//n
    return pl.pallas_call(full_kernel,grid=(chans//CT,),
        in_specs=[pl.BlockSpec((toks//BLOCK,BLOCK,CT),lambda c:(0,0,c)),pl.BlockSpec((toks,CT),lambda c:(0,c)),pl.BlockSpec((n,CT),lambda c:(0,c)),
                  pl.BlockSpec(outc.shape,lambda c:(0,0)),pl.BlockSpec(inc.shape,lambda c:(0,0)),pl.BlockSpec((1,CT),lambda c:(0,c))]
                 +[pl.BlockSpec(m.shape,lambda c:(0,0)) for m in msgs],
        out_specs=pl.BlockSpec((toks,CT),lambda c:(0,c)),
        out_shape=jax.ShapeDtypeStruct((toks,chans),bf16),
        scratch_shapes=[pltpu.VMEM((toks,n,LANES),f32),pltpu.VMEM((toks//BLOCK,BLOCK,CT),f32),pltpu.VMEM((toks//BLOCK,2*BLOCK,BLOCK*n),bf16),
                        pltpu.VMEM((BLOCK*n,CT),bf16),pltpu.VMEM((len(msgs),n,1,width),f32)],
        compiler_params=pltpu.CompilerParams(vmem_limit_bytes=VMEM_BYTES),
        name="full_pass")(step,g,decay,outc,inc,skip.reshape(1,-1),*msgs)


def slot_rows(ids_ref, gate_ref, cot_ref, capacity):
    toks = ids_ref.shape[0]
    named = (ids_ref[...] == 0).astype(f32)
    chosen = jnp.sum(named, axis=1, keepdims=True)
    gate = jnp.sum(named * gate_ref[...], axis=1, keepdims=True)
    earlier = (
        lax.broadcasted_iota(jnp.int32, (toks, toks), 1) < lax.broadcasted_iota(jnp.int32, (toks, toks), 0)
    ).astype(bf16)
    before = jnp.dot(
        earlier, jnp.broadcast_to(chosen, (toks, LANES)).astype(bf16), preferred_element_type=f32
    )[:, :capacity]
    slots = lax.broadcasted_iota(jnp.int32, (toks, capacity), 1).astype(f32)
    pick = jnp.where((before == slots) & (chosen > 0.5), 1.0, 0.0).astype(bf16)
    weighted = (gate * cot_ref[...].astype(f32)).astype(bf16)
    return lax.dot_general(
        pick, weighted, (((0,), (0,)), ((), ())), preferred_element_type=f32
    ).astype(bf16)


def pack_kernel(masks, part, place_ref, ids_ref, gate_ref, cot_ref, hidden_ref, *rest):
    *outs, routed = rest
    hid, rows = hidden_ref.shape
    capacity = routed.shape[0]
    routed[...] = slot_rows(ids_ref, gate_ref, cot_ref, capacity)
    eye = (
        lax.broadcasted_iota(jnp.int32, (rows, rows), 0) == lax.broadcasted_iota(jnp.int32, (rows, rows), 1)
    ).astype(bf16)
    turned = lax.dot_general(
        eye, hidden_ref[...], (((1,), (1,)), ((), ())), preferred_element_type=f32
    ).astype(bf16)
    pair = place_ref[0] // 2
    for mask, out in zip(masks, outs):
        out[:, :hid] = turned
        target = (pair ^ (mask // 2)) * 2
        for core in range(2):
            lanes = pl.ds(pl.multiple_of((target + core) * part, LANES), part)
            out[core * capacity : (core + 1) * capacity, hid:] = routed[:, lanes]
        if 2 * capacity < rows:
            out[2 * capacity :, hid:] = jnp.zeros((rows - 2 * capacity, part), bf16)


def pack(place, ids, gate, cot, hidden, masks, part, capacity):
    hid, rows = hidden.shape
    whole = pl.BlockSpec(memory_space=pltpu.VMEM)
    return pl.pallas_call(
        functools.partial(pack_kernel, masks, part),
        in_specs=[pl.BlockSpec(memory_space=pltpu.SMEM)] + [whole] * 4,
        out_specs=[whole] * len(masks),
        out_shape=[jax.ShapeDtypeStruct((rows, hid + part), bf16)] * len(masks),
        scratch_shapes=[pltpu.VMEM((capacity, cot.shape[1]), bf16)],
        compiler_params=pltpu.CompilerParams(vmem_limit_bytes=VMEM_BYTES),
        name="pack",
    )(place, ids, gate, cot, hidden)


def mine_kernel(capacity, place_ref, *rest):
    *packs, out_ref = rest
    start = pl.multiple_of((place_ref[0] % 2) * capacity, capacity)
    for slot, block in enumerate(packs):
        out_ref[slot * capacity : (slot + 1) * capacity] = block[pl.ds(start, capacity), :]


def mine(place, packs, part, capacity):
    column = packs[0].shape[1] // part - 1
    return pl.pallas_call(
        functools.partial(mine_kernel, capacity),
        grid=(1,),
        in_specs=[pl.BlockSpec(memory_space=pltpu.SMEM)]
        + [pl.BlockSpec((2 * capacity, part), lambda c: (0, column))] * len(packs),
        out_specs=pl.BlockSpec((len(packs) * capacity, part), lambda c: (0, 0)),
        out_shape=jax.ShapeDtypeStruct((len(packs) * capacity, part), bf16),
        name="own_columns",
    )(place, *packs)


def weight_kernel(capacity, peers, place_ref, *rest):
    packs = rest[:peers]
    *parts, out_ref, rows_ref = rest[peers:]
    count = len(parts)
    rows = count * capacity

    @pl.when(pl.program_id(0) == 0)
    def _():
        for ahead, piece in enumerate(parts):
            block = lax.rem(place_ref[1] + ahead, count)
            for slot in range(peers):
                start = pl.multiple_of(slot * rows + block * capacity, capacity)
                rows_ref[pl.ds(start, capacity), :] = piece[slot * capacity : (slot + 1) * capacity]

    hidden = jnp.concatenate([block[...] for block in packs], axis=0)
    out_ref[...] = lax.dot_general(
        rows_ref[...], hidden, (((0,), (0,)), ((), ())), preferred_element_type=f32
    )


def weight_grad(place, packs, parts, part, capacity):
    peers = len(packs)
    rows = packs[0].shape[0]
    hid = packs[0].shape[1] - part
    step = hid // 2 if hid % (2 * LANES) == 0 else hid
    return pl.pallas_call(
        functools.partial(weight_kernel, capacity, peers),
        grid=(hid // step,),
        in_specs=[pl.BlockSpec(memory_space=pltpu.SMEM)]
        + [pl.BlockSpec((rows, step), lambda c: (0, c))] * peers
        + [pl.BlockSpec(p.shape, lambda c: (0, 0)) for p in parts],
        out_specs=pl.BlockSpec((part, step), lambda c: (0, c)),
        out_shape=jax.ShapeDtypeStruct((part, hid), f32),
        scratch_shapes=[pltpu.VMEM((peers * rows, part), bf16)],
        compiler_params=pltpu.CompilerParams(vmem_limit_bytes=VMEM_BYTES),
        name="weight_grad",
    )(place, *packs, *parts)


def routed_kernel(ids_ref, gate_ref, cot_ref, out_ref):
    out_ref[...] = slot_rows(ids_ref, gate_ref, cot_ref, out_ref.shape[0])


def routed_rows(ids, gate, cot, capacity):
    return pl.pallas_call(
        routed_kernel,
        out_shape=jax.ShapeDtypeStruct((capacity, cot.shape[1]), bf16),
        name="routed_rows",
    )(ids, gate, cot)


def from_ahead(value, axis, by):
    peers = lax.axis_size(axis)
    return lax.ppermute(value, axis, [(i, i - by) for i in range(by, peers)])


def around(value, axis, by):
    peers = lax.axis_size(axis)
    return lax.ppermute(value, axis, [(i, (i - by) % peers) for i in range(peers)])


def across(value, axis, mask):
    return lax.ppermute(value, axis, [(i, i ^ mask) for i in range(lax.axis_size(axis))])


def on_device(
    cotangent,
    expert_ids,
    gate_probs,
    hidden_acts,
    step_input,
    step_proj,
    step_bias,
    decay_rate,
    input_coef,
    output_coef,
    grad_output,
    skip_weight,
):
    peers = lax.axis_size("dp")
    spans = lax.axis_size("seq")
    hid, rows = hidden_acts.shape
    features = cotangent.shape[2]
    capacity = rows // spans
    part = features // peers
    place = jnp.stack([lax.axis_index("dp"), lax.axis_index("seq")]).astype(jnp.int32)
    gathers = (
        peers * rows * 2 < features * 4
        and peers & (peers - 1) == 0
        and peers > 1
        and part % LANES == 0
        and hid % part == 0
        and 2 * capacity <= rows
    )
    if gathers:
        masks = list(range(0, peers, 2))
        sent = pack(place, expert_ids[0], gate_probs[0], cotangent[0], hidden_acts, masks, part, capacity)
        near = [sent[0]] + [across(v, "dp", m) for v, m in zip(sent[1:], masks[1:])]

    step, message = state_pass(
        step_input[0], step_proj, step_bias, decay_rate, output_coef[0], grad_output[0]
    )
    messages = [from_ahead(message, "seq", by) for by in range(1, spans)]

    if gathers:
        packs = near + [across(v, "dp", 1) for v in near]
        own = mine(place, packs, part, capacity)
        parts = [own] + [around(own, "seq", by) for by in range(1, spans)]
        grad_down = weight_grad(place, packs, parts, part, capacity)
    else:
        routed = routed_rows(expert_ids[0], gate_probs[0], cotangent[0], capacity)
        dense = lax.dot_general(
            lax.all_gather(routed, "seq", axis=0, tiled=True),
            hidden_acts,
            (((0,), (1,)), ((), ())),
            preferred_element_type=f32,
        )
        grad_down = lax.psum_scatter(dense, "dp", scatter_dimension=0, tiled=True)

    grad_x = full_pass(
        step, grad_output[0], decay_rate, output_coef[0], input_coef[0], skip_weight, messages
    )[None]
    return (grad_down, grad_x)


def solution(mesh):
    return jax.shard_map(
        on_device,
        mesh=mesh,
        in_specs=(
            P("dp", "seq", None),
            P("dp", "seq", None),
            P("dp", "seq", None),
            P("seq", "dp"),
            P("dp", "seq", None),
            P(),
            P(),
            P(),
            P("dp", None, "seq"),
            P("dp", None, "seq"),
            P("dp", "seq", None),
            P(),
        ),
        out_specs=(P("dp", "seq"), P("dp", "seq", None)),
        check_vma=False,
    )
```

```python
import functools
import math

import jax
import jax.numpy as jnp
from jax import lax
from jax.experimental import pallas as pl
from jax.experimental.pallas import tpu as pltpu
from jax.sharding import PartitionSpec as P

LANES = 128
BLOCK = 16
CT = 1024
CARRY_CT = 512
STATE_CT = 512
PREP_CT = 2048
HALF = 8
VMEM_BYTES = 32 * 2**20
LOG2E = math.log2(math.e)
f32 = jnp.float32
bf16 = jnp.bfloat16
WHOLE = pl.BlockSpec(memory_space=pltpu.VMEM)


def work(micros):
    return pl.CostEstimate(flops=micros * 10**7, bytes_accessed=micros * 10**4, transcendentals=0)


def softplus(v):
    return jnp.maximum(v, 0.0) + jnp.log1p(jnp.exp(-jnp.abs(v)))


def halves(v):
    high = v.astype(bf16)
    return high, (v - high.astype(f32)).astype(bf16)


def fill_picks(inc_ref, picks, token_major):
    n, toks = inc_ref.shape
    span = BLOCK * n
    col = lax.broadcasted_iota(jnp.int32, (toks, span), 1)
    state_of = lax.broadcasted_iota(jnp.int32, (n, span), 1)
    if token_major:
        own, state_of = col // n, state_of % n
    else:
        own, state_of = col % BLOCK, state_of // BLOCK
    own = own == lax.broadcasted_iota(jnp.int32, (toks, span), 0) % BLOCK
    sel = (state_of == lax.broadcasted_iota(jnp.int32, (n, span), 0)).astype(bf16)
    for part, vals in enumerate(halves(inc_ref[...])):
        wide = lax.dot_general(vals, sel, (((0,), (0,)), ((), ())), preferred_element_type=f32)
        wide = jnp.where(own, wide, 0.0).astype(bf16)
        for b in range(toks // BLOCK):
            picks[b, part * BLOCK : (part + 1) * BLOCK, :] = wide[b * BLOCK : (b + 1) * BLOCK]


def state_kernel(masks, part, place_ref, *rest):
    count = 10 if masks else 6
    sources, rest = rest[:count], rest[count:]
    (step_ref, later_ref, msg_ref, g_out, decay_out), rest = rest[:5], rest[5:]
    packs, rest = rest[: len(masks)], rest[len(masks) :]
    fetched, rest = rest[: count - 2], rest[count - 2 :]
    fetched = (*fetched[:-2], decay_out, *fetched[-2:], g_out)
    coef, sums, upto, terms0, terms1, tots, routed, small, wide = rest
    x_ref, bias_ref, decay_ref, outc_ref, proj_ref, g_ref = fetched[-6:]
    toks, chans = g_ref.shape
    n = decay_ref.shape[0]
    width = chans // n
    chunk = STATE_CT
    chunks = chans // chunk
    preps = chans // PREP_CT
    copies = [pltpu.make_async_copy(sources[k], fetched[k], small.at[k]) for k in range(count - 2)]
    for copy in copies:
        copy.start()
    columns = []
    for c in range(preps):
        at = slice(c * PREP_CT, (c + 1) * PREP_CT)
        columns.append(
            [
                pltpu.make_async_copy(sources[k].at[:, at], fetched[k].at[:, at], wide.at[k - count + 2, c])
                for k in (count - 2, count - 1)
            ]
        )
        for copy in columns[-1]:
            copy.start()

    row = lax.broadcasted_iota(jnp.int32, (toks, toks), 0)
    col = lax.broadcasted_iota(jnp.int32, (toks, toks), 1)
    for half in range(2):
        lanes = slice(half * toks, (half + 1) * toks)
        sums[:toks, lanes] = (col <= row).astype(bf16)
        sums[toks:, lanes] = (col > row).astype(bf16)
    for copy in copies:
        copy.wait()
    if masks:
        fill_packs(masks, part, place_ref, *fetched[:4], packs, routed)
    rows = lax.broadcasted_iota(jnp.int32, (n, toks), 0)
    for half, vals in enumerate(halves(outc_ref[...])):
        for m in range(n):
            coef[half * n : (half + 1) * n, m * toks : (m + 1) * toks] = jnp.where(
                rows == m, vals, jnp.zeros_like(vals)
            )

    for c in range(preps):
        at = slice(c * PREP_CT, (c + 1) * PREP_CT)
        for copy in columns[c]:
            copy.wait()
        step = softplus(jnp.dot(x_ref[...], proj_ref[:, at], preferred_element_type=f32) + bias_ref[:, at])
        step_ref[:, at] = step
        both = jnp.dot(sums[...], jnp.concatenate(halves(step), axis=0), preferred_element_type=f32)
        upto[:, at] = both[:toks].astype(bf16)
        later_ref[:, at] = both[toks:].astype(bf16)
        tots[:, at] = both[toks - 1 : toks]

    for c in range(chunks + 1):
        for m in range(n):
            if c < chunks:
                at = slice(c * chunk, (c + 1) * chunk)
                rate = jnp.broadcast_to(decay_ref[m : m + 1, at] * (-LOG2E), (BLOCK, chunk)).astype(bf16)
                for d in range(toks // BLOCK):
                    here = slice(d * BLOCK, (d + 1) * BLOCK)
                    (terms0, terms1)[c % 2][m * toks + d * BLOCK : m * toks + (d + 1) * BLOCK, :] = (
                        jnp.exp2(upto[here, at] * rate) * g_ref[here, at]
                    )
        if c > 0:
            at = slice((c - 1) * chunk, c * chunk)
            both = jnp.dot(coef[...], (terms0, terms1)[(c - 1) % 2][...], preferred_element_type=f32)
            msg_ref[:, at] = (both[:n] + both[n:]).astype(bf16)
    total = jnp.concatenate([tots[:, k * width : (k + 1) * width] for k in range(n)], axis=0)
    high, low = halves(total)
    msg_ref[:, chans : chans + width] = high
    msg_ref[:, chans + width : chans + 2 * width] = low


def state_pass(x, proj, bias, decay, outc, g, place, expert, masks, part, capacity):
    toks, chans = g.shape
    n = decay.shape[0]
    width = chans // n
    sources = [*expert, x, bias.reshape(1, -1), decay, outc, proj, g]
    kept = [v for v in sources if v is not decay and v is not g]
    if masks:
        rows, hid = expert[3].shape
        packed = [jax.ShapeDtypeStruct((rows, hid + part), bf16)] * len(masks)
        routed = (capacity, expert[2].shape[1])
    else:
        packed, routed = [], (BLOCK, LANES)
    return pl.pallas_call(
        functools.partial(state_kernel, masks, part),
        in_specs=[pl.BlockSpec(memory_space=pltpu.SMEM)] + [pl.BlockSpec(memory_space=pl.ANY)] * len(sources),
        out_specs=[WHOLE] * (5 + len(packed)),
        out_shape=[
            jax.ShapeDtypeStruct((toks, chans), f32),
            jax.ShapeDtypeStruct((toks, chans), bf16),
            jax.ShapeDtypeStruct((n, chans + 2 * width), bf16),
            jax.ShapeDtypeStruct(g.shape, g.dtype),
            jax.ShapeDtypeStruct(decay.shape, decay.dtype),
        ]
        + packed,
        scratch_shapes=[pltpu.VMEM(v.shape, v.dtype) for v in kept]
        + [
            pltpu.VMEM((2 * n, n * toks), bf16),
            pltpu.VMEM((2 * toks, 2 * toks), bf16),
            pltpu.VMEM((toks, chans), bf16),
            pltpu.VMEM((n * toks, STATE_CT), bf16),
            pltpu.VMEM((n * toks, STATE_CT), bf16),
            pltpu.VMEM((1, chans), f32),
            pltpu.VMEM(routed, bf16),
            pltpu.SemaphoreType.DMA((len(sources) - 2,)),
            pltpu.SemaphoreType.DMA((2, chans // PREP_CT)),
        ],
        compiler_params=pltpu.CompilerParams(vmem_limit_bytes=56 * 2**20),
        cost_estimate=work(8),
        name="state_pass",
    )(place, *sources)


def local_kernel(step_ref, decay_ref, outc_ref, inc_ref, skip_ref, g_ref, out_ref, outb, picks, step3, g3, adjs):
    toks, chans = g_ref.shape
    n = decay_ref.shape[0]
    tiles = CT // LANES
    blocks = toks // BLOCK
    vals = outc_ref[...]
    for t in range(toks):
        outb[t] = jnp.broadcast_to(vals[:, t : t + 1], (n, LANES))
    fill_picks(inc_ref, picks, True)

    for c in range(chans // CT):
        lanes = slice(c * CT, (c + 1) * CT)
        step3[...] = step_ref[:, lanes].reshape(blocks, BLOCK, CT)
        g3[...] = g_ref[:, lanes].astype(f32).reshape(blocks, BLOCK, CT)
        rate = [decay_ref[:, c * CT + q * LANES : c * CT + (q + 1) * LANES] * (-LOG2E) for q in range(tiles)]

        def body(i, states):
            b = blocks - 1 - i
            states = list(states)
            for k in reversed(range(BLOCK)):
                ob = outb[b * BLOCK + k]
                for q in range(tiles):
                    sl = slice(q * LANES, (q + 1) * LANES)
                    s = jnp.broadcast_to(step3[b, k : k + 1, sl], (n, LANES))
                    g = jnp.broadcast_to(g3[b, k : k + 1, sl], (n, LANES))
                    adj = states[q] + ob * g
                    adjs[b, k * n : (k + 1) * n, sl] = adj.astype(bf16)
                    states[q] = jnp.exp2(s * rate[q]) * adj
            return tuple(states)

        lax.fori_loop(0, blocks, body, tuple(jnp.zeros((n, LANES), f32) for _ in range(tiles)))
        for b in range(blocks):
            both = jnp.dot(picks[b], adjs[b], preferred_element_type=f32)
            y = both[:BLOCK] + both[BLOCK:]
            rows = slice(b * BLOCK, (b + 1) * BLOCK)
            out_ref[rows, lanes] = step_ref[rows, lanes] * y + skip_ref[:, lanes] * g_ref[rows, lanes].astype(f32)


def local_pass(step, decay, outc, inc, skip, g):
    toks, chans = g.shape
    n = decay.shape[0]
    blocks = toks // BLOCK
    return pl.pallas_call(
        local_kernel,
        in_specs=[WHOLE] * 6,
        out_specs=WHOLE,
        out_shape=jax.ShapeDtypeStruct((toks, chans), f32),
        scratch_shapes=[
            pltpu.VMEM((toks, n, LANES), f32),
            pltpu.VMEM((blocks, 2 * BLOCK, BLOCK * n), bf16),
            pltpu.VMEM((blocks, BLOCK, CT), f32),
            pltpu.VMEM((blocks, BLOCK, CT), f32),
            pltpu.VMEM((blocks, BLOCK * n, CT), bf16),
        ],
        compiler_params=pltpu.CompilerParams(vmem_limit_bytes=VMEM_BYTES),
        cost_estimate=work(13),
        name="local_pass",
    )(step, decay, outc, inc, skip.reshape(1, -1), g)


def carry_kernel(local_ref, step_ref, later_ref, decay_ref, inc_ref, *rest):
    *msgs, out_ref, picks, terms0, terms1 = rest
    toks, chans = step_ref.shape
    n = decay_ref.shape[0]
    width = chans // n
    blocks = toks // BLOCK
    chunk = CARRY_CT
    fill_picks(inc_ref, picks, False)
    totals = [
        msg[:, chans : chans + width].astype(f32) + msg[:, chans + width : chans + 2 * width].astype(f32)
        for msg in msgs[:-1]
    ]

    chunks = chans // chunk

    def prepare(c):
        lanes = slice(c * chunk, (c + 1) * chunk)
        rate = decay_ref[:, lanes] * (-LOG2E)
        state = msgs[-1][:, lanes].astype(f32)
        for k in reversed(range(len(msgs) - 1)):
            at = c * chunk
            total = [totals[k][(at + j) // width : (at + j) // width + 1, (at + j) % width : (at + j) % width + LANES] for j in range(0, chunk, LANES)]
            total = jnp.concatenate(total, axis=1)
            state = msgs[k][:, lanes].astype(f32) + jnp.exp2(total * rate) * state
        return rate, state

    for c in range(chunks + 1):
        if c < chunks:
            rate, state = prepare(c)
            terms = (terms0, terms1)[c % 2]
            lanes = slice(c * chunk, (c + 1) * chunk)
            later = later_ref[:, lanes]
        for b in range(blocks):
            if c < chunks:
                for m in range(b * n // blocks, (b + 1) * n // blocks):
                    spread_rate = jnp.broadcast_to(rate[m : m + 1], (BLOCK, chunk)).astype(bf16)
                    spread_state = jnp.broadcast_to(state[m : m + 1], (BLOCK, chunk)).astype(bf16)
                    for d in range(blocks):
                        terms[d, m * BLOCK : (m + 1) * BLOCK, :] = (
                            jnp.exp2(later[d * BLOCK : (d + 1) * BLOCK] * spread_rate) * spread_state
                        )
            if c > 0:
                done = (terms0, terms1)[(c - 1) % 2]
                at = slice((c - 1) * chunk, c * chunk)
                both = jnp.dot(picks[b], done[b], preferred_element_type=f32)
                rows = slice(b * BLOCK, (b + 1) * BLOCK)
                out_ref[rows, at] = (
                    local_ref[rows, at] + step_ref[rows, at] * (both[:BLOCK] + both[BLOCK:])
                ).astype(bf16)


def carry_pass(local, step, later, decay, inc, msgs):
    toks, chans = step.shape
    n = decay.shape[0]
    blocks = toks // BLOCK
    return pl.pallas_call(
        carry_kernel,
        in_specs=[WHOLE] * (5 + len(msgs)),
        out_specs=WHOLE,
        out_shape=jax.ShapeDtypeStruct((toks, chans), bf16),
        scratch_shapes=[
            pltpu.VMEM((blocks, 2 * BLOCK, BLOCK * n), bf16),
            pltpu.VMEM((blocks, BLOCK * n, CARRY_CT), bf16),
            pltpu.VMEM((blocks, BLOCK * n, CARRY_CT), bf16),
        ],
        compiler_params=pltpu.CompilerParams(vmem_limit_bytes=VMEM_BYTES),
        cost_estimate=work(6),
        name="carry_pass",
    )(local, step, later, decay, inc, *msgs)


def slot_rows(ids_ref, gate_ref, cot_ref, capacity):
    toks = ids_ref.shape[1]
    named = (ids_ref[...] == 0).astype(f32)
    chosen = jnp.broadcast_to(jnp.sum(named, axis=0, keepdims=True), (capacity, toks))
    gate = jnp.sum(named * gate_ref[...], axis=0, keepdims=True)
    earlier = (
        lax.broadcasted_iota(jnp.int32, (toks, toks), 0) < lax.broadcasted_iota(jnp.int32, (toks, toks), 1)
    ).astype(bf16)
    before = jnp.dot(chosen.astype(bf16), earlier, preferred_element_type=f32)
    slots = lax.broadcasted_iota(jnp.int32, (capacity, toks), 0).astype(f32)
    pick = jnp.where((before == slots) & (chosen > 0.5), 1.0, 0.0)
    weight = jnp.sum(pick * gate, axis=1, keepdims=True)
    rows = jnp.dot(pick.astype(bf16), cot_ref[...], preferred_element_type=f32)
    return (weight * rows).astype(bf16)


def fill_packs(masks, part, place_ref, ids_ref, gate_ref, cot_ref, hidden_ref, outs, routed):
    rows, hid = hidden_ref.shape
    capacity = routed.shape[0]
    routed[...] = slot_rows(ids_ref, gate_ref, cot_ref, capacity)
    pair = place_ref[0] // 2
    for mask, out in zip(masks, outs):
        out[:, :hid] = hidden_ref[...]
        target = (pair ^ (mask // 2)) * 2
        for core in range(2):
            lanes = pl.ds(pl.multiple_of((target + core) * part, LANES), part)
            out[core * capacity : (core + 1) * capacity, hid:] = routed[:, lanes]
        if 2 * capacity < rows:
            out[2 * capacity :, hid:] = jnp.zeros((rows - 2 * capacity, part), bf16)


def mine_kernel(capacity, place_ref, *rest):
    *packs, out_ref = rest
    start = pl.multiple_of((place_ref[0] % 2) * capacity, capacity)
    part = out_ref.shape[1]
    for slot, block in enumerate(packs):
        hid = block.shape[1] - part
        out_ref[slot * capacity : (slot + 1) * capacity] = block[pl.ds(start, capacity), hid:]


def mine(place, packs, part, capacity):
    return pl.pallas_call(
        functools.partial(mine_kernel, capacity),
        in_specs=[pl.BlockSpec(memory_space=pltpu.SMEM)] + [WHOLE] * len(packs),
        out_specs=WHOLE,
        out_shape=jax.ShapeDtypeStruct((len(packs) * capacity, part), bf16),
        compiler_params=pltpu.CompilerParams(vmem_limit_bytes=2 * 2**20),
        cost_estimate=work(1),
        name="own_columns",
    )(place, *packs)


def weight_kernel(capacity, peers, place_ref, *rest):
    packs = rest[:peers]
    *parts, out_ref, rows_ref = rest[peers:]
    count = len(parts)
    rows = count * capacity

    @pl.when(pl.program_id(0) == 0)
    def _():
        for ahead, piece in enumerate(parts):
            block = lax.rem(place_ref[1] + ahead, count)
            for slot in range(peers):
                start = pl.multiple_of(slot * rows + block * capacity, capacity)
                rows_ref[pl.ds(start, capacity), :] = piece[slot * capacity : (slot + 1) * capacity]

    hidden = jnp.concatenate([block[...] for block in packs], axis=0)
    out_ref[...] = lax.dot_general(
        rows_ref[...], hidden, (((0,), (0,)), ((), ())), preferred_element_type=f32
    )


def weight_grad(place, packs, parts, part, capacity):
    peers = len(packs)
    rows = packs[0].shape[0]
    hid = packs[0].shape[1] - part
    step = hid // 2 if hid % (2 * LANES) == 0 else hid
    return pl.pallas_call(
        functools.partial(weight_kernel, capacity, peers),
        grid=(hid // step,),
        in_specs=[pl.BlockSpec(memory_space=pltpu.SMEM)]
        + [pl.BlockSpec((rows, step), lambda c: (0, c))] * peers
        + [pl.BlockSpec(p.shape, lambda c: (0, 0)) for p in parts],
        out_specs=pl.BlockSpec((part, step), lambda c: (0, c)),
        out_shape=jax.ShapeDtypeStruct((part, hid), f32),
        scratch_shapes=[pltpu.VMEM((peers * rows, part), bf16)],
        compiler_params=pltpu.CompilerParams(vmem_limit_bytes=16 * 2**20),
        cost_estimate=work(3),
        name="weight_grad",
    )(place, *packs, *parts)


def routed_kernel(ids_ref, gate_ref, cot_ref, out_ref):
    out_ref[...] = slot_rows(ids_ref, gate_ref, cot_ref, out_ref.shape[0])


def routed_rows(ids, gate, cot, capacity):
    return pl.pallas_call(
        routed_kernel,
        out_shape=jax.ShapeDtypeStruct((capacity, cot.shape[1]), bf16),
        compiler_params=pltpu.CompilerParams(vmem_limit_bytes=8 * 2**20),
        cost_estimate=work(1),
        name="routed_rows",
    )(ids, gate, cot)


def from_ahead(value, axis, by):
    peers = lax.axis_size(axis)
    return lax.ppermute(value, axis, [(i, i - by) for i in range(by, peers)])


def around(value, axis, by):
    peers = lax.axis_size(axis)
    return lax.ppermute(value, axis, [(i, (i - by) % peers) for i in range(peers)])


def across(value, axis, mask):
    return lax.ppermute(value, axis, [(i, i ^ mask) for i in range(lax.axis_size(axis))])


def on_device(
    cotangent,
    expert_ids,
    gate_probs,
    hidden_acts,
    step_input,
    step_proj,
    step_bias,
    decay_rate,
    input_coef,
    output_coef,
    grad_output,
    skip_weight,
):
    peers = lax.axis_size("dp")
    spans = lax.axis_size("seq")
    hid, rows = hidden_acts.shape
    features = cotangent.shape[2]
    capacity = rows // spans
    part = features // peers
    place = jnp.stack([lax.axis_index("dp"), lax.axis_index("seq")]).astype(jnp.int32)
    gathers = (
        peers * rows * 2 < features * 4
        and peers & (peers - 1) == 0
        and peers > 1
        and part % LANES == 0
        and hid % part == 0
        and 2 * capacity <= rows
    )
    masks = list(range(0, peers, 2)) if gathers else []
    expert = [expert_ids[0].T, gate_probs[0].T, cotangent[0], hidden_acts.T] if gathers else []
    step, later, message, grad, decay, *sent = state_pass(
        step_input[0],
        step_proj,
        step_bias,
        decay_rate,
        output_coef[0],
        grad_output[0],
        place,
        expert,
        masks,
        part,
        capacity,
    )
    messages = [from_ahead(message, "seq", by) for by in range(1, spans)]
    if gathers:
        near = [sent[0]] + [across(v, "dp", m) for v, m in zip(sent[1:], masks[1:])]
    local = local_pass(step, decay, output_coef[0], input_coef[0], skip_weight, grad)

    if gathers:
        far, local, messages = lax.optimization_barrier((near[1:], local, messages))
        near = near[:1] + list(far)
        packs = near + [across(v, "dp", 1) for v in near]
        own = mine(place, packs, part, capacity)
        parts = [own] + [around(own, "seq", by) for by in range(1, spans)]
        grad_down = weight_grad(place, packs, parts, part, capacity)
    else:
        routed = routed_rows(expert_ids[0].T, gate_probs[0].T, cotangent[0], capacity)
        dense = lax.dot_general(
            lax.all_gather(routed, "seq", axis=0, tiled=True),
            hidden_acts,
            (((0,), (1,)), ((), ())),
            preferred_element_type=f32,
        )
        grad_down = lax.psum_scatter(dense, "dp", scatter_dimension=0, tiled=True)

    grad_x = carry_pass(local, step, later, decay, input_coef[0], messages)[None]
    return (grad_down, grad_x)


def solution(mesh):
    return jax.shard_map(
        on_device,
        mesh=mesh,
        in_specs=(
            P("dp", "seq", None),
            P("dp", "seq", None),
            P("dp", "seq", None),
            P("seq", "dp"),
            P("dp", "seq", None),
            P(),
            P(),
            P(),
            P("dp", None, "seq"),
            P("dp", None, "seq"),
            P("dp", "seq", None),
            P(),
        ),
        out_specs=(P("dp", "seq"), P("dp", "seq", None)),
        check_vma=False,
    )
```

```python
import functools
import math

import jax
import jax.numpy as jnp
from jax import lax
from jax.experimental import pallas as pl
from jax.experimental.pallas import tpu as pltpu
from jax.sharding import PartitionSpec as P

LANES = 128
BLOCK = 16
CT = 1024
CARRY_CT = 512
STATE_CT = 512
PREP_CT = 2048
HALF = 8
VMEM_BYTES = 32 * 2**20
LOG2E = math.log2(math.e)
f32 = jnp.float32
bf16 = jnp.bfloat16
WHOLE = pl.BlockSpec(memory_space=pltpu.VMEM)


def work(micros):
    return pl.CostEstimate(flops=micros * 10**7, bytes_accessed=micros * 10**4, transcendentals=0)


def softplus(v):
    return jnp.maximum(v, 0.0) + jnp.log1p(jnp.exp(-jnp.abs(v)))


def halves(v):
    high = v.astype(bf16)
    return high, (v - high.astype(f32)).astype(bf16)


def fill_picks(inc_ref, picks, token_major):
    n, toks = inc_ref.shape
    span = BLOCK * n
    col = lax.broadcasted_iota(jnp.int32, (toks, span), 1)
    state_of = lax.broadcasted_iota(jnp.int32, (n, span), 1)
    if token_major:
        own, state_of = col // n, state_of % n
    else:
        own, state_of = col % BLOCK, state_of // BLOCK
    own = own == lax.broadcasted_iota(jnp.int32, (toks, span), 0) % BLOCK
    sel = (state_of == lax.broadcasted_iota(jnp.int32, (n, span), 0)).astype(bf16)
    for part, vals in enumerate(halves(inc_ref[...])):
        wide = lax.dot_general(vals, sel, (((0,), (0,)), ((), ())), preferred_element_type=f32)
        wide = jnp.where(own, wide, 0.0).astype(bf16)
        for b in range(toks // BLOCK):
            picks[b, part * BLOCK : (part + 1) * BLOCK, :] = wide[b * BLOCK : (b + 1) * BLOCK]


def state_kernel(masks, part, *rest):
    count = 10 if masks else 6
    sources, rest = rest[:count], rest[count:]
    (step_ref, later_ref, msg_ref), rest = rest[:3], rest[3:]
    packs, rest = rest[: len(masks)], rest[len(masks) :]
    fetched, rest = rest[:count], rest[count:]
    coef, sums, upto, terms0, terms1, tots, routed, small, wide = rest
    x_ref, bias_ref, decay_ref, outc_ref, proj_ref, g_ref = fetched[-6:]
    toks, chans = g_ref.shape
    n = decay_ref.shape[0]
    width = chans // n
    chunk = STATE_CT
    chunks = chans // chunk
    preps = chans // PREP_CT
    copies = [pltpu.make_async_copy(sources[k], fetched[k], small.at[k]) for k in range(count - 2)]
    for copy in copies:
        copy.start()
    columns = []
    for c in range(preps):
        at = slice(c * PREP_CT, (c + 1) * PREP_CT)
        columns.append(
            [
                pltpu.make_async_copy(sources[k].at[:, at], fetched[k].at[:, at], wide.at[k - count + 2, c])
                for k in (count - 2, count - 1)
            ]
        )
        for copy in columns[-1]:
            copy.start()

    row = lax.broadcasted_iota(jnp.int32, (toks, toks), 0)
    col = lax.broadcasted_iota(jnp.int32, (toks, toks), 1)
    for half in range(2):
        lanes = slice(half * toks, (half + 1) * toks)
        sums[:toks, lanes] = (col <= row).astype(bf16)
        sums[toks:, lanes] = (col > row).astype(bf16)
    for copy in copies:
        copy.wait()
    if masks:
        fill_packs(masks, part, *fetched[:4], packs, routed)
    rows = lax.broadcasted_iota(jnp.int32, (n, toks), 0)
    for half, vals in enumerate(halves(outc_ref[...])):
        for m in range(n):
            coef[half * n : (half + 1) * n, m * toks : (m + 1) * toks] = jnp.where(
                rows == m, vals, jnp.zeros_like(vals)
            )

    for c in range(chunks + 1):
        if c < chunks and c * chunk % PREP_CT == 0:
            p = c * chunk // PREP_CT
            at = slice(p * PREP_CT, (p + 1) * PREP_CT)
            for copy in columns[p]:
                copy.wait()
            step = softplus(jnp.dot(x_ref[...], proj_ref[:, at], preferred_element_type=f32) + bias_ref[:, at])
            step_ref[:, at] = step
            both = jnp.dot(sums[...], jnp.concatenate(halves(step), axis=0), preferred_element_type=f32)
            upto[:, at] = both[:toks].astype(bf16)
            later_ref[:, at] = both[toks:].astype(bf16)
            tots[:, at] = both[toks - 1 : toks]
        for m in range(n):
            if c < chunks:
                at = slice(c * chunk, (c + 1) * chunk)
                rate = jnp.broadcast_to(decay_ref[m : m + 1, at] * (-LOG2E), (BLOCK, chunk)).astype(bf16)
                for d in range(toks // BLOCK):
                    here = slice(d * BLOCK, (d + 1) * BLOCK)
                    (terms0, terms1)[c % 2][m * toks + d * BLOCK : m * toks + (d + 1) * BLOCK, :] = (
                        jnp.exp2(upto[here, at] * rate) * g_ref[here, at]
                    )
        if c > 0:
            at = slice((c - 1) * chunk, c * chunk)
            both = jnp.dot(coef[...], (terms0, terms1)[(c - 1) % 2][...], preferred_element_type=f32)
            msg_ref[:, at] = (both[:n] + both[n:]).astype(bf16)
    total = jnp.concatenate([tots[:, k * width : (k + 1) * width] for k in range(n)], axis=0)
    high, low = halves(total)
    msg_ref[:, chans : chans + width] = high
    msg_ref[:, chans + width : chans + 2 * width] = low


def state_pass(x, proj, bias, decay, outc, g, expert, masks, part, capacity):
    toks, chans = g.shape
    n = decay.shape[0]
    width = chans // n
    sources = [*expert, x, bias.reshape(1, -1), decay, outc, proj, g]
    if masks:
        rows, hid = expert[3].shape
        packed = [jax.ShapeDtypeStruct((rows, hid + part), bf16)] * len(masks)
        routed = (capacity, expert[2].shape[1])
    else:
        packed, routed = [], (BLOCK, LANES)
    return pl.pallas_call(
        functools.partial(state_kernel, masks, part),
        in_specs=[pl.BlockSpec(memory_space=pl.ANY)] * len(sources),
        out_specs=[WHOLE] * (3 + len(packed)),
        out_shape=[
            jax.ShapeDtypeStruct((toks, chans), f32),
            jax.ShapeDtypeStruct((toks, chans), bf16),
            jax.ShapeDtypeStruct((n, chans + 2 * width), bf16),
        ]
        + packed,
        scratch_shapes=[pltpu.VMEM(v.shape, v.dtype) for v in sources]
        + [
            pltpu.VMEM((2 * n, n * toks), bf16),
            pltpu.VMEM((2 * toks, 2 * toks), bf16),
            pltpu.VMEM((toks, chans), bf16),
            pltpu.VMEM((n * toks, STATE_CT), bf16),
            pltpu.VMEM((n * toks, STATE_CT), bf16),
            pltpu.VMEM((1, chans), f32),
            pltpu.VMEM(routed, bf16),
            pltpu.SemaphoreType.DMA((len(sources) - 2,)),
            pltpu.SemaphoreType.DMA((2, chans // PREP_CT)),
        ],
        compiler_params=pltpu.CompilerParams(vmem_limit_bytes=58 * 2**20),
        cost_estimate=work(8),
        name="state_pass",
    )(*sources)


def local_kernel(step_ref, decay_ref, outc_ref, inc_ref, skip_ref, g_ref, out_ref, outb, picks, step3, g3, adjs):
    toks, chans = g_ref.shape
    n = decay_ref.shape[0]
    tiles = CT // LANES
    blocks = toks // BLOCK
    vals = outc_ref[...]
    for t in range(toks):
        outb[t] = jnp.broadcast_to(vals[:, t : t + 1], (n, LANES))
    fill_picks(inc_ref, picks, True)

    for c in range(chans // CT):
        lanes = slice(c * CT, (c + 1) * CT)
        step3[...] = step_ref[:, lanes].reshape(blocks, BLOCK, CT)
        g3[...] = g_ref[:, lanes].astype(f32).reshape(blocks, BLOCK, CT)
        rate = [decay_ref[:, c * CT + q * LANES : c * CT + (q + 1) * LANES] * (-LOG2E) for q in range(tiles)]

        def body(i, states):
            b = blocks - 1 - i
            states = list(states)
            for k in reversed(range(BLOCK)):
                ob = outb[b * BLOCK + k]
                for q in range(tiles):
                    sl = slice(q * LANES, (q + 1) * LANES)
                    s = jnp.broadcast_to(step3[b, k : k + 1, sl], (n, LANES))
                    g = jnp.broadcast_to(g3[b, k : k + 1, sl], (n, LANES))
                    adj = states[q] + ob * g
                    adjs[b, k * n : (k + 1) * n, sl] = adj.astype(bf16)
                    states[q] = jnp.exp2(s * rate[q]) * adj
            return tuple(states)

        lax.fori_loop(0, blocks, body, tuple(jnp.zeros((n, LANES), f32) for _ in range(tiles)))
        for b in range(blocks):
            both = jnp.dot(picks[b], adjs[b], preferred_element_type=f32)
            y = both[:BLOCK] + both[BLOCK:]
            rows = slice(b * BLOCK, (b + 1) * BLOCK)
            out_ref[rows, lanes] = step_ref[rows, lanes] * y + skip_ref[:, lanes] * g_ref[rows, lanes].astype(f32)


def local_pass(step, decay, outc, inc, skip, g):
    toks, chans = g.shape
    n = decay.shape[0]
    blocks = toks // BLOCK
    return pl.pallas_call(
        local_kernel,
        in_specs=[WHOLE] * 6,
        out_specs=WHOLE,
        out_shape=jax.ShapeDtypeStruct((toks, chans), f32),
        scratch_shapes=[
            pltpu.VMEM((toks, n, LANES), f32),
            pltpu.VMEM((blocks, 2 * BLOCK, BLOCK * n), bf16),
            pltpu.VMEM((blocks, BLOCK, CT), f32),
            pltpu.VMEM((blocks, BLOCK, CT), f32),
            pltpu.VMEM((blocks, BLOCK * n, CT), bf16),
        ],
        compiler_params=pltpu.CompilerParams(vmem_limit_bytes=VMEM_BYTES),
        cost_estimate=work(13),
        name="local_pass",
    )(step, decay, outc, inc, skip.reshape(1, -1), g)


def carry_kernel(local_ref, step_ref, later_ref, decay_ref, inc_ref, *rest):
    *msgs, out_ref, picks, terms0, terms1 = rest
    toks, chans = step_ref.shape
    n = decay_ref.shape[0]
    width = chans // n
    blocks = toks // BLOCK
    chunk = CARRY_CT
    fill_picks(inc_ref, picks, False)
    totals = [
        msg[:, chans : chans + width].astype(f32) + msg[:, chans + width : chans + 2 * width].astype(f32)
        for msg in msgs[:-1]
    ]

    chunks = chans // chunk

    def prepare(c):
        lanes = slice(c * chunk, (c + 1) * chunk)
        rate = decay_ref[:, lanes] * (-LOG2E)
        state = msgs[-1][:, lanes].astype(f32)
        for k in reversed(range(len(msgs) - 1)):
            at = c * chunk
            total = [totals[k][(at + j) // width : (at + j) // width + 1, (at + j) % width : (at + j) % width + LANES] for j in range(0, chunk, LANES)]
            total = jnp.concatenate(total, axis=1)
            state = msgs[k][:, lanes].astype(f32) + jnp.exp2(total * rate) * state
        return rate, state

    for c in range(chunks + 1):
        if c < chunks:
            rate, state = prepare(c)
            terms = (terms0, terms1)[c % 2]
            lanes = slice(c * chunk, (c + 1) * chunk)
            later = later_ref[:, lanes]
        for b in range(blocks):
            if c < chunks:
                for m in range(b * n // blocks, (b + 1) * n // blocks):
                    spread_rate = jnp.broadcast_to(rate[m : m + 1], (BLOCK, chunk)).astype(bf16)
                    spread_state = jnp.broadcast_to(state[m : m + 1], (BLOCK, chunk)).astype(bf16)
                    for d in range(blocks):
                        terms[d, m * BLOCK : (m + 1) * BLOCK, :] = (
                            jnp.exp2(later[d * BLOCK : (d + 1) * BLOCK] * spread_rate) * spread_state
                        )
            if c > 0:
                done = (terms0, terms1)[(c - 1) % 2]
                at = slice((c - 1) * chunk, c * chunk)
                both = jnp.dot(picks[b], done[b], preferred_element_type=f32)
                rows = slice(b * BLOCK, (b + 1) * BLOCK)
                out_ref[rows, at] = (
                    local_ref[rows, at] + step_ref[rows, at] * (both[:BLOCK] + both[BLOCK:])
                ).astype(bf16)


def carry_pass(local, step, later, decay, inc, msgs):
    toks, chans = step.shape
    n = decay.shape[0]
    blocks = toks // BLOCK
    return pl.pallas_call(
        carry_kernel,
        in_specs=[WHOLE] * (5 + len(msgs)),
        out_specs=WHOLE,
        out_shape=jax.ShapeDtypeStruct((toks, chans), bf16),
        scratch_shapes=[
            pltpu.VMEM((blocks, 2 * BLOCK, BLOCK * n), bf16),
            pltpu.VMEM((blocks, BLOCK * n, CARRY_CT), bf16),
            pltpu.VMEM((blocks, BLOCK * n, CARRY_CT), bf16),
        ],
        compiler_params=pltpu.CompilerParams(vmem_limit_bytes=VMEM_BYTES),
        cost_estimate=work(6),
        name="carry_pass",
    )(local, step, later, decay, inc, *msgs)


def slot_rows(ids_ref, gate_ref, cot_ref, capacity):
    toks = ids_ref.shape[1]
    named = (ids_ref[...] == 0).astype(f32)
    chosen = jnp.broadcast_to(jnp.sum(named, axis=0, keepdims=True), (capacity, toks))
    gate = jnp.sum(named * gate_ref[...], axis=0, keepdims=True)
    earlier = (
        lax.broadcasted_iota(jnp.int32, (toks, toks), 0) < lax.broadcasted_iota(jnp.int32, (toks, toks), 1)
    ).astype(bf16)
    before = jnp.dot(chosen.astype(bf16), earlier, preferred_element_type=f32)
    slots = lax.broadcasted_iota(jnp.int32, (capacity, toks), 0).astype(f32)
    pick = jnp.where((before == slots) & (chosen > 0.5), 1.0, 0.0)
    weight = jnp.sum(pick * gate, axis=1, keepdims=True)
    rows = jnp.dot(pick.astype(bf16), cot_ref[...], preferred_element_type=f32)
    return (weight * rows).astype(bf16)


def fill_packs(masks, part, ids_ref, gate_ref, cot_ref, hidden_ref, outs, routed):
    rows, hid = hidden_ref.shape
    capacity = routed.shape[0]
    routed[...] = slot_rows(ids_ref, gate_ref, cot_ref, capacity)
    pair = lax.axis_index("dp") // 2
    for mask, out in zip(masks, outs):
        out[:, :hid] = hidden_ref[...]
        target = (pair ^ (mask // 2)) * 2
        for core in range(2):
            lanes = pl.ds(pl.multiple_of((target + core) * part, LANES), part)
            out[core * capacity : (core + 1) * capacity, hid:] = routed[:, lanes]
        if 2 * capacity < rows:
            out[2 * capacity :, hid:] = jnp.zeros((rows - 2 * capacity, part), bf16)


def mine_kernel(capacity, *rest):
    *packs, out_ref = rest
    start = pl.multiple_of((lax.axis_index("dp") % 2) * capacity, capacity)
    part = out_ref.shape[1]
    for slot, block in enumerate(packs):
        hid = block.shape[1] - part
        out_ref[slot * capacity : (slot + 1) * capacity] = block[pl.ds(start, capacity), hid:]


def mine(packs, part, capacity):
    return pl.pallas_call(
        functools.partial(mine_kernel, capacity),
        in_specs=[WHOLE] * len(packs),
        out_specs=WHOLE,
        out_shape=jax.ShapeDtypeStruct((len(packs) * capacity, part), bf16),
        compiler_params=pltpu.CompilerParams(vmem_limit_bytes=2 * 2**20),
        cost_estimate=work(1),
        name="own_columns",
    )(*packs)


def weight_kernel(capacity, peers, step, *rest):
    packs = rest[:peers]
    *parts, out_ref, rows_ref = rest[peers:]
    count = len(parts)
    rows = count * capacity

    @pl.when(pl.program_id(0) == 0)
    def _():
        for ahead, piece in enumerate(parts):
            block = lax.axis_index("seq") ^ ahead
            for slot in range(peers):
                start = pl.multiple_of(slot * rows + block * capacity, capacity)
                rows_ref[pl.ds(start, capacity), :] = piece[slot * capacity : (slot + 1) * capacity]

    lanes = pl.ds(pl.multiple_of(pl.program_id(0) * step, LANES), step)
    hidden = jnp.concatenate([block[:, lanes] for block in packs], axis=0)
    out_ref[...] = lax.dot_general(
        rows_ref[...], hidden, (((0,), (0,)), ((), ())), preferred_element_type=f32
    )


def weight_grad(packs, parts, part, capacity):
    peers = len(packs)
    rows = packs[0].shape[0]
    hid = packs[0].shape[1] - part
    step = hid // 2 if hid % (2 * LANES) == 0 else hid
    return pl.pallas_call(
        functools.partial(weight_kernel, capacity, peers, step),
        grid=(hid // step,),
        in_specs=[WHOLE] * (peers + len(parts)),
        out_specs=pl.BlockSpec((part, step), lambda c: (0, c)),
        out_shape=jax.ShapeDtypeStruct((part, hid), f32),
        scratch_shapes=[pltpu.VMEM((peers * rows, part), bf16)],
        compiler_params=pltpu.CompilerParams(vmem_limit_bytes=16 * 2**20),
        cost_estimate=work(3),
        name="weight_grad",
    )(*packs, *parts)


def routed_kernel(ids_ref, gate_ref, cot_ref, out_ref):
    out_ref[...] = slot_rows(ids_ref, gate_ref, cot_ref, out_ref.shape[0])


def routed_rows(ids, gate, cot, capacity):
    return pl.pallas_call(
        routed_kernel,
        out_shape=jax.ShapeDtypeStruct((capacity, cot.shape[1]), bf16),
        compiler_params=pltpu.CompilerParams(vmem_limit_bytes=8 * 2**20),
        cost_estimate=work(1),
        name="routed_rows",
    )(ids, gate, cot)


def from_ahead(value, axis, by):
    peers = lax.axis_size(axis)
    return lax.ppermute(value, axis, [(i, i - by) for i in range(by, peers)])


def across(value, axis, mask):
    return lax.ppermute(value, axis, [(i, i ^ mask) for i in range(lax.axis_size(axis))])


def on_device(
    cotangent,
    expert_ids,
    gate_probs,
    hidden_acts,
    step_input,
    step_proj,
    step_bias,
    decay_rate,
    input_coef,
    output_coef,
    grad_output,
    skip_weight,
):
    peers = lax.axis_size("dp")
    spans = lax.axis_size("seq")
    hid, rows = hidden_acts.shape
    features = cotangent.shape[2]
    capacity = rows // spans
    part = features // peers
    gathers = (
        peers * rows * 2 < features * 4
        and peers & (peers - 1) == 0
        and spans & (spans - 1) == 0
        and peers > 1
        and part % LANES == 0
        and hid % part == 0
        and 2 * capacity <= rows
    )
    masks = list(range(0, peers, 2)) if gathers else []
    expert = [expert_ids[0].T, gate_probs[0].T, cotangent[0], hidden_acts.T] if gathers else []
    step, later, message, *sent = state_pass(
        step_input[0],
        step_proj,
        step_bias,
        decay_rate,
        output_coef[0],
        grad_output[0],
        expert,
        masks,
        part,
        capacity,
    )
    messages = [from_ahead(message, "seq", by) for by in range(1, spans)]
    if gathers:
        near = [sent[0]] + [across(v, "dp", m) for v, m in zip(sent[1:], masks[1:])]
    local = local_pass(step, decay_rate, output_coef[0], input_coef[0], skip_weight, grad_output[0])

    if gathers:
        far, local, messages = lax.optimization_barrier((near[1:], local, messages))
        near = near[:1] + list(far)
        packs = near + [across(v, "dp", 1) for v in near]
        own = mine(packs, part, capacity)
        parts = [own] + [across(own, "seq", by) for by in range(1, spans)]
        grad_down = weight_grad(packs, parts, part, capacity)
    else:
        routed = routed_rows(expert_ids[0].T, gate_probs[0].T, cotangent[0], capacity)
        dense = lax.dot_general(
            lax.all_gather(routed, "seq", axis=0, tiled=True),
            hidden_acts,
            (((0,), (1,)), ((), ())),
            preferred_element_type=f32,
        )
        grad_down = lax.psum_scatter(dense, "dp", scatter_dimension=0, tiled=True)

    grad_x = carry_pass(local, step, later, decay_rate, input_coef[0], messages)[None]
    return (grad_down, grad_x)


def solution(mesh):
    return jax.shard_map(
        on_device,
        mesh=mesh,
        in_specs=(
            P("dp", "seq", None),
            P("dp", "seq", None),
            P("dp", "seq", None),
            P("seq", "dp"),
            P("dp", "seq", None),
            P(),
            P(),
            P(),
            P("dp", None, "seq"),
            P("dp", None, "seq"),
            P("dp", "seq", None),
            P(),
        ),
        out_specs=(P("dp", "seq"), P("dp", "seq", None)),
        check_vma=False,
    )
```

```python
import functools
import math

import jax
import jax.numpy as jnp
from jax import lax
from jax.experimental import pallas as pl
from jax.experimental.pallas import tpu as pltpu
from jax.sharding import PartitionSpec as P

LANES = 128
BLOCK = 16
CT = 1024
CARRY_CT = 256
STATE_CT = 512
PREP_CT = 2048
HALF = 8
VMEM_BYTES = 32 * 2**20
LOG2E = math.log2(math.e)
f32 = jnp.float32
bf16 = jnp.bfloat16
WHOLE = pl.BlockSpec(memory_space=pltpu.VMEM)


def work(micros):
    return pl.CostEstimate(flops=micros * 10**7, bytes_accessed=micros * 10**4, transcendentals=0)


def softplus(v):
    return jnp.maximum(v, 0.0) + jnp.log1p(jnp.exp(-jnp.abs(v)))


def halves(v):
    high = v.astype(bf16)
    return high, (v - high.astype(f32)).astype(bf16)


def fill_picks(inc_ref, picks, token_major):
    n, toks = inc_ref.shape
    span = BLOCK * n
    col = lax.broadcasted_iota(jnp.int32, (toks, span), 1)
    state_of = lax.broadcasted_iota(jnp.int32, (n, span), 1)
    if token_major:
        own, state_of = col // n, state_of % n
    else:
        own, state_of = col % BLOCK, state_of // BLOCK
    own = own == lax.broadcasted_iota(jnp.int32, (toks, span), 0) % BLOCK
    sel = (state_of == lax.broadcasted_iota(jnp.int32, (n, span), 0)).astype(bf16)
    for part, vals in enumerate(halves(inc_ref[...])):
        wide = lax.dot_general(vals, sel, (((0,), (0,)), ((), ())), preferred_element_type=f32)
        wide = jnp.where(own, wide, 0.0).astype(bf16)
        for b in range(toks // BLOCK):
            picks[b, part * BLOCK : (part + 1) * BLOCK, :] = wide[b * BLOCK : (b + 1) * BLOCK]


def state_kernel(masks, part, *rest):
    count = 10 if masks else 6
    sources, rest = rest[:count], rest[count:]
    (step_ref, later_ref, msg_ref), rest = rest[:3], rest[3:]
    packs, rest = rest[: len(masks)], rest[len(masks) :]
    fetched, rest = rest[:count], rest[count:]
    coef, sums, upto, terms0, terms1, tots, routed, small, wide = rest
    x_ref, bias_ref, decay_ref, outc_ref, proj_ref, g_ref = fetched[-6:]
    toks, chans = g_ref.shape
    n = decay_ref.shape[0]
    width = chans // n
    chunk = STATE_CT
    chunks = chans // chunk
    preps = chans // PREP_CT
    copies = [pltpu.make_async_copy(sources[k], fetched[k], small.at[k]) for k in range(count - 2)]
    for copy in copies:
        copy.start()
    columns = []
    for c in range(preps):
        at = slice(c * PREP_CT, (c + 1) * PREP_CT)
        columns.append(
            [
                pltpu.make_async_copy(sources[k].at[:, at], fetched[k].at[:, at], wide.at[k - count + 2, c])
                for k in (count - 2, count - 1)
            ]
        )
        for copy in columns[-1]:
            copy.start()

    row = lax.broadcasted_iota(jnp.int32, (toks, toks), 0)
    col = lax.broadcasted_iota(jnp.int32, (toks, toks), 1)
    for half in range(2):
        sums[:, half * toks : (half + 1) * toks] = (col <= row).astype(bf16)
    for copy in copies:
        copy.wait()
    if masks:
        fill_packs(masks, part, *fetched[:4], packs, routed)
    rows = lax.broadcasted_iota(jnp.int32, (n, toks), 0)
    for half, vals in enumerate(halves(outc_ref[...])):
        for m in range(n):
            coef[half * n : (half + 1) * n, m * toks : (m + 1) * toks] = jnp.where(
                rows == m, vals, jnp.zeros_like(vals)
            )

    for c in range(chunks + 1):
        if c < chunks and c * chunk % PREP_CT == 0:
            p = c * chunk // PREP_CT
            at = slice(p * PREP_CT, (p + 1) * PREP_CT)
            for copy in columns[p]:
                copy.wait()
            step = softplus(jnp.dot(x_ref[...], proj_ref[:, at], preferred_element_type=f32) + bias_ref[:, at])
            step_ref[:, at] = step
            summed = jnp.dot(sums[...], jnp.concatenate(halves(step), axis=0), preferred_element_type=f32)
            total = summed[toks - 1 : toks]
            upto[:, at] = summed.astype(bf16)
            later_ref[:, at] = (total - summed).astype(bf16)
            tots[:, at] = total
        for m in range(n):
            if c < chunks:
                at = slice(c * chunk, (c + 1) * chunk)
                rate = jnp.broadcast_to(decay_ref[m : m + 1, at] * (-LOG2E), (BLOCK, chunk)).astype(bf16)
                for d in range(toks // BLOCK):
                    here = slice(d * BLOCK, (d + 1) * BLOCK)
                    (terms0, terms1)[c % 2][m * toks + d * BLOCK : m * toks + (d + 1) * BLOCK, :] = (
                        jnp.exp2(upto[here, at] * rate) * g_ref[here, at]
                    )
        if c > 0:
            at = slice((c - 1) * chunk, c * chunk)
            both = jnp.dot(coef[...], (terms0, terms1)[(c - 1) % 2][...], preferred_element_type=f32)
            msg_ref[:, at] = (both[:n] + both[n:]).astype(bf16)
    total = jnp.concatenate([tots[:, k * width : (k + 1) * width] for k in range(n)], axis=0)
    high, low = halves(total)
    msg_ref[:, chans : chans + width] = high
    msg_ref[:, chans + width : chans + 2 * width] = low


def state_pass(x, proj, bias, decay, outc, g, expert, masks, part, capacity):
    toks, chans = g.shape
    n = decay.shape[0]
    width = chans // n
    sources = [*expert, x, bias.reshape(1, -1), decay, outc, proj, g]
    if masks:
        rows, hid = expert[3].shape
        packed = [jax.ShapeDtypeStruct((rows, hid + part), bf16)] * len(masks)
        routed = (capacity, expert[2].shape[1])
    else:
        packed, routed = [], (BLOCK, LANES)
    return pl.pallas_call(
        functools.partial(state_kernel, masks, part),
        in_specs=[pl.BlockSpec(memory_space=pl.ANY)] * len(sources),
        out_specs=[WHOLE] * (3 + len(packed)),
        out_shape=[
            jax.ShapeDtypeStruct((toks, chans), f32),
            jax.ShapeDtypeStruct((toks, chans), bf16),
            jax.ShapeDtypeStruct((n, chans + 2 * width), bf16),
        ]
        + packed,
        scratch_shapes=[pltpu.VMEM(v.shape, v.dtype) for v in sources]
        + [
            pltpu.VMEM((2 * n, n * toks), bf16),
            pltpu.VMEM((toks, 2 * toks), bf16),
            pltpu.VMEM((toks, chans), bf16),
            pltpu.VMEM((n * toks, STATE_CT), bf16),
            pltpu.VMEM((n * toks, STATE_CT), bf16),
            pltpu.VMEM((1, chans), f32),
            pltpu.VMEM(routed, bf16),
            pltpu.SemaphoreType.DMA((len(sources) - 2,)),
            pltpu.SemaphoreType.DMA((2, chans // PREP_CT)),
        ],
        compiler_params=pltpu.CompilerParams(vmem_limit_bytes=58 * 2**20),
        cost_estimate=work(8),
        name="state_pass",
    )(*sources)


def local_kernel(step_ref, decay_ref, outc_ref, inc_ref, skip_ref, g_ref, out_ref, outb, picks, g3, adjs):
    toks, chans = g_ref.shape
    n = decay_ref.shape[0]
    tiles = CT // LANES
    blocks = toks // BLOCK
    vals = outc_ref[...]
    for t in range(toks):
        outb[t] = jnp.broadcast_to(vals[:, t : t + 1], (n, LANES))
    fill_picks(inc_ref, picks, True)

    for c in range(chans // CT):
        lanes = slice(c * CT, (c + 1) * CT)
        g3[...] = g_ref[:, lanes].astype(f32).reshape(blocks, BLOCK, CT)
        rate = [decay_ref[:, c * CT + q * LANES : c * CT + (q + 1) * LANES] * (-LOG2E) for q in range(tiles)]

        def body(i, states):
            b = blocks - 1 - i
            states = list(states)
            for k in reversed(range(BLOCK)):
                ob = outb[b * BLOCK + k]
                for q in range(tiles):
                    sl = slice(q * LANES, (q + 1) * LANES)
                    s = jnp.broadcast_to(
                        step_ref[b, k : k + 1, c * CT + q * LANES : c * CT + (q + 1) * LANES], (n, LANES)
                    )
                    g = jnp.broadcast_to(g3[b, k : k + 1, sl], (n, LANES))
                    adj = states[q] + ob * g
                    adjs[b, k * n : (k + 1) * n, sl] = adj.astype(bf16)
                    states[q] = jnp.exp2(s * rate[q]) * adj
            return tuple(states)

        lax.fori_loop(0, blocks, body, tuple(jnp.zeros((n, LANES), f32) for _ in range(tiles)))
        for b in range(blocks):
            both = jnp.dot(picks[b], adjs[b], preferred_element_type=f32)
            y = both[:BLOCK] + both[BLOCK:]
            rows = slice(b * BLOCK, (b + 1) * BLOCK)
            out_ref[rows, lanes] = step_ref[b, :, lanes] * y + skip_ref[:, lanes] * g_ref[rows, lanes].astype(f32)


def local_pass(step, decay, outc, inc, skip, g):
    toks, chans = g.shape
    n = decay.shape[0]
    blocks = toks // BLOCK
    return pl.pallas_call(
        local_kernel,
        in_specs=[WHOLE] * 6,
        out_specs=WHOLE,
        out_shape=jax.ShapeDtypeStruct((toks, chans), f32),
        scratch_shapes=[
            pltpu.VMEM((toks, n, LANES), f32),
            pltpu.VMEM((blocks, 2 * BLOCK, BLOCK * n), bf16),
            pltpu.VMEM((blocks, BLOCK, CT), f32),
            pltpu.VMEM((blocks, BLOCK * n, CT), bf16),
        ],
        compiler_params=pltpu.CompilerParams(vmem_limit_bytes=VMEM_BYTES),
        cost_estimate=work(13),
        name="local_pass",
    )(step.reshape(blocks, BLOCK, chans), decay, outc, inc, skip.reshape(1, -1), g)


def carry_kernel(local_ref, step_ref, later_ref, decay_ref, inc_ref, *rest):
    *msgs, out_ref, picks, terms0, terms1 = rest
    toks, chans = step_ref.shape
    n = decay_ref.shape[0]
    width = chans // n
    blocks = toks // BLOCK
    chunk = CARRY_CT
    fill_picks(inc_ref, picks, False)
    totals = [
        msg[:, chans : chans + width].astype(f32) + msg[:, chans + width : chans + 2 * width].astype(f32)
        for msg in msgs[:-1]
    ]

    chunks = chans // chunk

    def prepare(c):
        lanes = slice(c * chunk, (c + 1) * chunk)
        rate = decay_ref[:, lanes] * (-LOG2E)
        state = msgs[-1][:, lanes].astype(f32)
        for k in reversed(range(len(msgs) - 1)):
            at = c * chunk
            total = [totals[k][(at + j) // width : (at + j) // width + 1, (at + j) % width : (at + j) % width + LANES] for j in range(0, chunk, LANES)]
            total = jnp.concatenate(total, axis=1)
            state = msgs[k][:, lanes].astype(f32) + jnp.exp2(total * rate) * state
        return rate, state

    for c in range(chunks + 1):
        if c < chunks:
            rate, state = prepare(c)
            terms = (terms0, terms1)[c % 2]
            lanes = slice(c * chunk, (c + 1) * chunk)
            later = later_ref[:, lanes]
        for b in range(blocks):
            if c < chunks:
                for m in range(b * n // blocks, (b + 1) * n // blocks):
                    spread_rate = jnp.broadcast_to(rate[m : m + 1], (BLOCK, chunk)).astype(bf16)
                    spread_state = jnp.broadcast_to(state[m : m + 1], (BLOCK, chunk)).astype(bf16)
                    for d in range(blocks):
                        terms[d, m * BLOCK : (m + 1) * BLOCK, :] = (
                            jnp.exp2(later[d * BLOCK : (d + 1) * BLOCK] * spread_rate) * spread_state
                        )
            if c > 0:
                done = (terms0, terms1)[(c - 1) % 2]
                at = slice((c - 1) * chunk, c * chunk)
                both = jnp.dot(picks[b], done[b], preferred_element_type=f32)
                rows = slice(b * BLOCK, (b + 1) * BLOCK)
                out_ref[rows, at] = (
                    local_ref[rows, at] + step_ref[rows, at] * (both[:BLOCK] + both[BLOCK:])
                ).astype(bf16)


def carry_pass(local, step, later, decay, inc, msgs):
    toks, chans = step.shape
    n = decay.shape[0]
    blocks = toks // BLOCK
    return pl.pallas_call(
        carry_kernel,
        in_specs=[WHOLE] * (5 + len(msgs)),
        out_specs=WHOLE,
        out_shape=jax.ShapeDtypeStruct((toks, chans), bf16),
        scratch_shapes=[
            pltpu.VMEM((blocks, 2 * BLOCK, BLOCK * n), bf16),
            pltpu.VMEM((blocks, BLOCK * n, CARRY_CT), bf16),
            pltpu.VMEM((blocks, BLOCK * n, CARRY_CT), bf16),
        ],
        compiler_params=pltpu.CompilerParams(vmem_limit_bytes=VMEM_BYTES),
        cost_estimate=work(6),
        name="carry_pass",
    )(local, step, later, decay, inc, *msgs)


def slot_rows(ids_ref, gate_ref, cot_ref, capacity):
    toks = ids_ref.shape[1]
    named = (ids_ref[...] == 0).astype(f32)
    chosen = jnp.broadcast_to(jnp.sum(named, axis=0, keepdims=True), (capacity, toks))
    gate = jnp.sum(named * gate_ref[...], axis=0, keepdims=True)
    earlier = (
        lax.broadcasted_iota(jnp.int32, (toks, toks), 0) < lax.broadcasted_iota(jnp.int32, (toks, toks), 1)
    ).astype(bf16)
    before = jnp.dot(chosen.astype(bf16), earlier, preferred_element_type=f32)
    slots = lax.broadcasted_iota(jnp.int32, (capacity, toks), 0).astype(f32)
    pick = jnp.where((before == slots) & (chosen > 0.5), 1.0, 0.0)
    weight = jnp.sum(pick * gate, axis=1, keepdims=True)
    rows = jnp.dot(pick.astype(bf16), cot_ref[...], preferred_element_type=f32)
    return (weight * rows).astype(bf16)


def fill_packs(masks, part, ids_ref, gate_ref, cot_ref, hidden_ref, outs, routed):
    rows, hid = hidden_ref.shape
    capacity = routed.shape[0]
    routed[...] = slot_rows(ids_ref, gate_ref, cot_ref, capacity)
    pair = lax.axis_index("dp") // 2
    for mask, out in zip(masks, outs):
        out[:, :hid] = hidden_ref[...]
        target = (pair ^ (mask // 2)) * 2
        for core in range(2):
            lanes = pl.ds(pl.multiple_of((target + core) * part, LANES), part)
            out[core * capacity : (core + 1) * capacity, hid:] = routed[:, lanes]
        if 2 * capacity < rows:
            out[2 * capacity :, hid:] = jnp.zeros((rows - 2 * capacity, part), bf16)


def mine_kernel(capacity, *rest):
    *packs, out_ref = rest
    start = pl.multiple_of((lax.axis_index("dp") % 2) * capacity, capacity)
    part = out_ref.shape[1]
    for slot, block in enumerate(packs):
        hid = block.shape[1] - part
        out_ref[slot * capacity : (slot + 1) * capacity] = block[pl.ds(start, capacity), hid:]


def mine(packs, part, capacity):
    return pl.pallas_call(
        functools.partial(mine_kernel, capacity),
        in_specs=[WHOLE] * len(packs),
        out_specs=WHOLE,
        out_shape=jax.ShapeDtypeStruct((len(packs) * capacity, part), bf16),
        compiler_params=pltpu.CompilerParams(vmem_limit_bytes=2 * 2**20),
        cost_estimate=work(1),
        name="own_columns",
    )(*packs)


def weight_kernel(capacity, peers, step, *rest):
    packs = rest[:peers]
    *parts, out_ref, rows_ref = rest[peers:]
    count = len(parts)
    rows = count * capacity

    @pl.when(pl.program_id(0) == 0)
    def _():
        for ahead, piece in enumerate(parts):
            block = lax.axis_index("seq") ^ ahead
            for slot in range(peers):
                start = pl.multiple_of(slot * rows + block * capacity, capacity)
                rows_ref[pl.ds(start, capacity), :] = piece[slot * capacity : (slot + 1) * capacity]

    lanes = pl.ds(pl.multiple_of(pl.program_id(0) * step, LANES), step)
    hidden = jnp.concatenate([block[:, lanes] for block in packs], axis=0)
    out_ref[...] = lax.dot_general(
        rows_ref[...], hidden, (((0,), (0,)), ((), ())), preferred_element_type=f32
    )


def weight_grad(packs, parts, part, capacity):
    peers = len(packs)
    rows = packs[0].shape[0]
    hid = packs[0].shape[1] - part
    step = hid // 2 if hid % (2 * LANES) == 0 else hid
    return pl.pallas_call(
        functools.partial(weight_kernel, capacity, peers, step),
        grid=(hid // step,),
        in_specs=[WHOLE] * (peers + len(parts)),
        out_specs=pl.BlockSpec((part, step), lambda c: (0, c)),
        out_shape=jax.ShapeDtypeStruct((part, hid), f32),
        scratch_shapes=[pltpu.VMEM((peers * rows, part), bf16)],
        compiler_params=pltpu.CompilerParams(vmem_limit_bytes=16 * 2**20),
        cost_estimate=work(3),
        name="weight_grad",
    )(*packs, *parts)


def routed_kernel(ids_ref, gate_ref, cot_ref, out_ref):
    out_ref[...] = slot_rows(ids_ref, gate_ref, cot_ref, out_ref.shape[0])


def routed_rows(ids, gate, cot, capacity):
    return pl.pallas_call(
        routed_kernel,
        out_shape=jax.ShapeDtypeStruct((capacity, cot.shape[1]), bf16),
        compiler_params=pltpu.CompilerParams(vmem_limit_bytes=8 * 2**20),
        cost_estimate=work(1),
        name="routed_rows",
    )(ids, gate, cot)


def from_ahead(value, axis, by):
    peers = lax.axis_size(axis)
    return lax.ppermute(value, axis, [(i, i - by) for i in range(by, peers)])


def across(value, axis, mask):
    return lax.ppermute(value, axis, [(i, i ^ mask) for i in range(lax.axis_size(axis))])


def on_device(
    cotangent,
    expert_ids,
    gate_probs,
    hidden_acts,
    step_input,
    step_proj,
    step_bias,
    decay_rate,
    input_coef,
    output_coef,
    grad_output,
    skip_weight,
):
    peers = lax.axis_size("dp")
    spans = lax.axis_size("seq")
    hid, rows = hidden_acts.shape
    features = cotangent.shape[2]
    capacity = rows // spans
    part = features // peers
    gathers = (
        peers * rows * 2 < features * 4
        and peers & (peers - 1) == 0
        and spans & (spans - 1) == 0
        and peers > 1
        and part % LANES == 0
        and hid % part == 0
        and 2 * capacity <= rows
    )
    masks = list(range(0, peers, 2)) if gathers else []
    expert = [expert_ids[0].T, gate_probs[0].T, cotangent[0], hidden_acts.T] if gathers else []
    step, later, message, *sent = state_pass(
        step_input[0],
        step_proj,
        step_bias,
        decay_rate,
        output_coef[0],
        grad_output[0],
        expert,
        masks,
        part,
        capacity,
    )
    messages = [from_ahead(message, "seq", by) for by in range(2, spans)]
    if gathers:
        near = [sent[0]] + [across(v, "dp", m) for v, m in zip(sent[1:], masks[1:])]
    local = local_pass(step, decay_rate, output_coef[0], input_coef[0], skip_weight, grad_output[0])

    if gathers:
        far, local, messages, message = lax.optimization_barrier((near[1:], local, messages, message))
        near = near[:1] + list(far)
        packs = near + [across(v, "dp", 1) for v in near]
        own = mine(packs, part, capacity)
        parts = [own] + [across(own, "seq", by) for by in range(1, spans)]
        grad_down = weight_grad(packs, parts, part, capacity)
    else:
        routed = routed_rows(expert_ids[0].T, gate_probs[0].T, cotangent[0], capacity)
        dense = lax.dot_general(
            lax.all_gather(routed, "seq", axis=0, tiled=True),
            hidden_acts,
            (((0,), (1,)), ((), ())),
            preferred_element_type=f32,
        )
        grad_down = lax.psum_scatter(dense, "dp", scatter_dimension=0, tiled=True)

    messages = [from_ahead(message, "seq", 1)] + list(messages)
    grad_x = carry_pass(local, step, later, decay_rate, input_coef[0], messages)[None]
    return (grad_down, grad_x)


def solution(mesh):
    return jax.shard_map(
        on_device,
        mesh=mesh,
        in_specs=(
            P("dp", "seq", None),
            P("dp", "seq", None),
            P("dp", "seq", None),
            P("seq", "dp"),
            P("dp", "seq", None),
            P(),
            P(),
            P(),
            P("dp", None, "seq"),
            P("dp", None, "seq"),
            P("dp", "seq", None),
            P(),
        ),
        out_specs=(P("dp", "seq"), P("dp", "seq", None)),
        check_vma=False,
    )
```

```python
import functools
import math

import jax
import jax.numpy as jnp
from jax import lax
from jax.experimental import pallas as pl
from jax.experimental.pallas import tpu as pltpu
from jax.sharding import PartitionSpec as P

LANES = 128
BLOCK = 16
CT = 1024
CARRY_CT = 256
STATE_CT = 256
PREP_CT = 2048
HALF = 8
VMEM_BYTES = 32 * 2**20
LOG2E = math.log2(math.e)
f32 = jnp.float32
bf16 = jnp.bfloat16
WHOLE = pl.BlockSpec(memory_space=pltpu.VMEM)


def work(micros):
    return pl.CostEstimate(flops=micros * 10**7, bytes_accessed=micros * 10**4, transcendentals=0)


def softplus(v):
    return jnp.maximum(v, 0.0) + jnp.log1p(jnp.exp(-jnp.abs(v)))


def halves(v):
    high = v.astype(bf16)
    return high, (v - high.astype(f32)).astype(bf16)


def fill_picks(inc_ref, picks, token_major):
    n, toks = inc_ref.shape
    span = BLOCK * n
    col = lax.broadcasted_iota(jnp.int32, (toks, span), 1)
    state_of = lax.broadcasted_iota(jnp.int32, (n, span), 1)
    if token_major:
        own, state_of = col // n, state_of % n
    else:
        own, state_of = col % BLOCK, state_of // BLOCK
    own = own == lax.broadcasted_iota(jnp.int32, (toks, span), 0) % BLOCK
    sel = (state_of == lax.broadcasted_iota(jnp.int32, (n, span), 0)).astype(bf16)
    for part, vals in enumerate(halves(inc_ref[...])):
        wide = lax.dot_general(vals, sel, (((0,), (0,)), ((), ())), preferred_element_type=f32)
        wide = jnp.where(own, wide, 0.0).astype(bf16)
        for b in range(toks // BLOCK):
            picks[b, part * BLOCK : (part + 1) * BLOCK, :] = wide[b * BLOCK : (b + 1) * BLOCK]


def state_kernel(masks, part, *rest):
    count = 10 if masks else 6
    sources, rest = rest[:count], rest[count:]
    (step_ref, later_ref, msg_ref), rest = rest[:3], rest[3:]
    packs, rest = rest[: len(masks)], rest[len(masks) :]
    fetched, rest = rest[:count], rest[count:]
    coef, sums, upto, terms0, terms1, tots, routed, small, wide = rest
    x_ref, bias_ref, decay_ref, outc_ref, proj_ref, g_ref = fetched[-6:]
    toks, chans = g_ref.shape
    n = decay_ref.shape[0]
    width = chans // n
    chunk = STATE_CT
    chunks = chans // chunk
    preps = chans // PREP_CT
    copies = [pltpu.make_async_copy(sources[k], fetched[k], small.at[k]) for k in range(count - 2)]
    for copy in copies:
        copy.start()
    columns = []
    for c in range(preps):
        at = slice(c * PREP_CT, (c + 1) * PREP_CT)
        columns.append(
            [
                pltpu.make_async_copy(sources[k].at[:, at], fetched[k].at[:, at], wide.at[k - count + 2, c])
                for k in (count - 2, count - 1)
            ]
        )
        for copy in columns[-1]:
            copy.start()

    row = lax.broadcasted_iota(jnp.int32, (toks, toks), 0)
    col = lax.broadcasted_iota(jnp.int32, (toks, toks), 1)
    for half in range(2):
        sums[:, half * toks : (half + 1) * toks] = (col <= row).astype(bf16)
    for copy in copies:
        copy.wait()
    if masks:
        fill_packs(masks, part, *fetched[:4], packs, routed)
    rows = lax.broadcasted_iota(jnp.int32, (n, toks), 0)
    for half, vals in enumerate(halves(outc_ref[...])):
        for m in range(n):
            coef[half * n : (half + 1) * n, m * toks : (m + 1) * toks] = jnp.where(
                rows == m, vals, jnp.zeros_like(vals)
            )

    for c in range(chunks + 1):
        if c < chunks and c * chunk % PREP_CT == 0:
            p = c * chunk // PREP_CT
            at = slice(p * PREP_CT, (p + 1) * PREP_CT)
            for copy in columns[p]:
                copy.wait()
            step = softplus(jnp.dot(x_ref[...], proj_ref[:, at], preferred_element_type=f32) + bias_ref[:, at])
            step_ref[:, at] = step
            summed = jnp.dot(sums[...], jnp.concatenate(halves(step), axis=0), preferred_element_type=f32)
            total = summed[toks - 1 : toks]
            upto[:, at] = summed.astype(bf16)
            later_ref[:, at] = (total - summed).astype(bf16)
            tots[:, at] = total
        for m in range(n):
            if c < chunks:
                at = slice(c * chunk, (c + 1) * chunk)
                rate = jnp.broadcast_to(decay_ref[m : m + 1, at] * (-LOG2E), (BLOCK, chunk)).astype(bf16)
                for d in range(toks // BLOCK):
                    here = slice(d * BLOCK, (d + 1) * BLOCK)
                    (terms0, terms1)[c % 2][m * toks + d * BLOCK : m * toks + (d + 1) * BLOCK, :] = (
                        jnp.exp2(upto[here, at] * rate) * g_ref[here, at]
                    )
        if c > 0:
            at = slice((c - 1) * chunk, c * chunk)
            both = jnp.dot(coef[...], (terms0, terms1)[(c - 1) % 2][...], preferred_element_type=f32)
            msg_ref[:, at] = (both[:n] + both[n:]).astype(bf16)
    total = jnp.concatenate([tots[:, k * width : (k + 1) * width] for k in range(n)], axis=0)
    high, low = halves(total)
    msg_ref[:, chans : chans + width] = high
    msg_ref[:, chans + width : chans + 2 * width] = low


def state_pass(x, proj, bias, decay, outc, g, expert, masks, part, capacity):
    toks, chans = g.shape
    n = decay.shape[0]
    width = chans // n
    sources = [*expert, x, bias.reshape(1, -1), decay, outc, proj, g]
    if masks:
        rows, hid = expert[3].shape
        packed = [jax.ShapeDtypeStruct((rows, hid + part), bf16)] * len(masks)
        routed = (capacity, expert[2].shape[1])
    else:
        packed, routed = [], (BLOCK, LANES)
    return pl.pallas_call(
        functools.partial(state_kernel, masks, part),
        in_specs=[pl.BlockSpec(memory_space=pl.ANY)] * len(sources),
        out_specs=[WHOLE] * (3 + len(packed)),
        out_shape=[
            jax.ShapeDtypeStruct((toks, chans), f32),
            jax.ShapeDtypeStruct((toks, chans), bf16),
            jax.ShapeDtypeStruct((n, chans + 2 * width), bf16),
        ]
        + packed,
        scratch_shapes=[pltpu.VMEM(v.shape, v.dtype) for v in sources]
        + [
            pltpu.VMEM((2 * n, n * toks), bf16),
            pltpu.VMEM((toks, 2 * toks), bf16),
            pltpu.VMEM((toks, chans), bf16),
            pltpu.VMEM((n * toks, STATE_CT), bf16),
            pltpu.VMEM((n * toks, STATE_CT), bf16),
            pltpu.VMEM((1, chans), f32),
            pltpu.VMEM(routed, bf16),
            pltpu.SemaphoreType.DMA((len(sources) - 2,)),
            pltpu.SemaphoreType.DMA((2, chans // PREP_CT)),
        ],
        compiler_params=pltpu.CompilerParams(vmem_limit_bytes=58 * 2**20),
        cost_estimate=work(8),
        name="state_pass",
    )(*sources)


def local_kernel(step_ref, decay_ref, outc_ref, inc_ref, skip_ref, g_ref, out_ref, outb, picks, g3, adjs):
    toks, chans = g_ref.shape
    n = decay_ref.shape[0]
    tiles = CT // LANES
    blocks = toks // BLOCK
    vals = outc_ref[...]
    for t in range(toks):
        outb[t] = jnp.broadcast_to(vals[:, t : t + 1], (n, LANES))
    fill_picks(inc_ref, picks, True)

    for c in range(chans // CT):
        lanes = slice(c * CT, (c + 1) * CT)
        g3[...] = g_ref[:, lanes].astype(f32).reshape(blocks, BLOCK, CT)
        rate = [decay_ref[:, c * CT + q * LANES : c * CT + (q + 1) * LANES] * (-LOG2E) for q in range(tiles)]

        def body(i, states):
            b = blocks - 1 - i
            states = list(states)
            for k in reversed(range(BLOCK)):
                ob = outb[b * BLOCK + k]
                for q in range(tiles):
                    sl = slice(q * LANES, (q + 1) * LANES)
                    s = jnp.broadcast_to(
                        step_ref[b, k : k + 1, c * CT + q * LANES : c * CT + (q + 1) * LANES], (n, LANES)
                    )
                    g = jnp.broadcast_to(g3[b, k : k + 1, sl], (n, LANES))
                    adj = states[q] + ob * g
                    adjs[b, k * n : (k + 1) * n, sl] = adj.astype(bf16)
                    states[q] = jnp.exp2(s * rate[q]) * adj
            return tuple(states)

        lax.fori_loop(0, blocks, body, tuple(jnp.zeros((n, LANES), f32) for _ in range(tiles)))
        for b in range(blocks):
            both = jnp.dot(picks[b], adjs[b], preferred_element_type=f32)
            y = both[:BLOCK] + both[BLOCK:]
            rows = slice(b * BLOCK, (b + 1) * BLOCK)
            out_ref[rows, lanes] = step_ref[b, :, lanes] * y + skip_ref[:, lanes] * g_ref[rows, lanes].astype(f32)


def local_pass(step, decay, outc, inc, skip, g):
    toks, chans = g.shape
    n = decay.shape[0]
    blocks = toks // BLOCK
    return pl.pallas_call(
        local_kernel,
        in_specs=[WHOLE] * 6,
        out_specs=WHOLE,
        out_shape=jax.ShapeDtypeStruct((toks, chans), f32),
        scratch_shapes=[
            pltpu.VMEM((toks, n, LANES), f32),
            pltpu.VMEM((blocks, 2 * BLOCK, BLOCK * n), bf16),
            pltpu.VMEM((blocks, BLOCK, CT), f32),
            pltpu.VMEM((blocks, BLOCK * n, CT), bf16),
        ],
        compiler_params=pltpu.CompilerParams(vmem_limit_bytes=VMEM_BYTES),
        cost_estimate=work(13),
        name="local_pass",
    )(step.reshape(blocks, BLOCK, chans), decay, outc, inc, skip.reshape(1, -1), g)


def carry_kernel(local_ref, step_ref, later_ref, decay_ref, inc_ref, *rest):
    *msgs, out_ref, picks, terms0, terms1 = rest
    toks, chans = step_ref.shape
    n = decay_ref.shape[0]
    width = chans // n
    blocks = toks // BLOCK
    chunk = CARRY_CT
    fill_picks(inc_ref, picks, False)
    totals = [
        msg[:, chans : chans + width].astype(f32) + msg[:, chans + width : chans + 2 * width].astype(f32)
        for msg in msgs[:-1]
    ]

    chunks = chans // chunk

    def prepare(c):
        lanes = slice(c * chunk, (c + 1) * chunk)
        rate = decay_ref[:, lanes] * (-LOG2E)
        state = msgs[-1][:, lanes].astype(f32)
        for k in reversed(range(len(msgs) - 1)):
            at = c * chunk
            total = [totals[k][(at + j) // width : (at + j) // width + 1, (at + j) % width : (at + j) % width + LANES] for j in range(0, chunk, LANES)]
            total = jnp.concatenate(total, axis=1)
            state = msgs[k][:, lanes].astype(f32) + jnp.exp2(total * rate) * state
        return rate, state

    for c in range(chunks + 1):
        if c < chunks:
            rate, state = prepare(c)
            terms = (terms0, terms1)[c % 2]
            lanes = slice(c * chunk, (c + 1) * chunk)
            later = later_ref[:, lanes]
        for b in range(blocks):
            if c < chunks:
                for m in range(b * n // blocks, (b + 1) * n // blocks):
                    spread_rate = jnp.broadcast_to(rate[m : m + 1], (BLOCK, chunk)).astype(bf16)
                    spread_state = jnp.broadcast_to(state[m : m + 1], (BLOCK, chunk)).astype(bf16)
                    for d in range(blocks):
                        terms[d, m * BLOCK : (m + 1) * BLOCK, :] = (
                            jnp.exp2(later[d * BLOCK : (d + 1) * BLOCK] * spread_rate) * spread_state
                        )
            if c > 0:
                done = (terms0, terms1)[(c - 1) % 2]
                at = slice((c - 1) * chunk, c * chunk)
                both = jnp.dot(picks[b], done[b], preferred_element_type=f32)
                rows = slice(b * BLOCK, (b + 1) * BLOCK)
                out_ref[rows, at] = (
                    local_ref[rows, at] + step_ref[rows, at] * (both[:BLOCK] + both[BLOCK:])
                ).astype(bf16)


def carry_pass(local, step, later, decay, inc, msgs):
    toks, chans = step.shape
    n = decay.shape[0]
    blocks = toks // BLOCK
    return pl.pallas_call(
        carry_kernel,
        in_specs=[WHOLE] * (5 + len(msgs)),
        out_specs=WHOLE,
        out_shape=jax.ShapeDtypeStruct((toks, chans), bf16),
        scratch_shapes=[
            pltpu.VMEM((blocks, 2 * BLOCK, BLOCK * n), bf16),
            pltpu.VMEM((blocks, BLOCK * n, CARRY_CT), bf16),
            pltpu.VMEM((blocks, BLOCK * n, CARRY_CT), bf16),
        ],
        compiler_params=pltpu.CompilerParams(vmem_limit_bytes=VMEM_BYTES),
        cost_estimate=work(6),
        name="carry_pass",
    )(local, step, later, decay, inc, *msgs)


def slot_rows(ids_ref, gate_ref, cot_ref, capacity):
    toks = ids_ref.shape[1]
    named = (ids_ref[...] == 0).astype(f32)
    chosen = jnp.broadcast_to(jnp.sum(named, axis=0, keepdims=True), (capacity, toks))
    gate = jnp.sum(named * gate_ref[...], axis=0, keepdims=True)
    earlier = (
        lax.broadcasted_iota(jnp.int32, (toks, toks), 0) < lax.broadcasted_iota(jnp.int32, (toks, toks), 1)
    ).astype(bf16)
    before = jnp.dot(chosen.astype(bf16), earlier, preferred_element_type=f32)
    slots = lax.broadcasted_iota(jnp.int32, (capacity, toks), 0).astype(f32)
    pick = jnp.where((before == slots) & (chosen > 0.5), 1.0, 0.0)
    weight = jnp.sum(pick * gate, axis=1, keepdims=True)
    rows = jnp.dot(pick.astype(bf16), cot_ref[...], preferred_element_type=f32)
    return (weight * rows).astype(bf16)


def fill_packs(masks, part, ids_ref, gate_ref, cot_ref, hidden_ref, outs, routed):
    rows, hid = hidden_ref.shape
    capacity = routed.shape[0]
    routed[...] = slot_rows(ids_ref, gate_ref, cot_ref, capacity)
    pair = lax.axis_index("dp") // 2
    for mask, out in zip(masks, outs):
        out[:, :hid] = hidden_ref[...]
        target = (pair ^ (mask // 2)) * 2
        for core in range(2):
            lanes = pl.ds(pl.multiple_of((target + core) * part, LANES), part)
            out[core * capacity : (core + 1) * capacity, hid:] = routed[:, lanes]
        if 2 * capacity < rows:
            out[2 * capacity :, hid:] = jnp.zeros((rows - 2 * capacity, part), bf16)


def mine_kernel(capacity, *rest):
    *packs, out_ref = rest
    start = pl.multiple_of((lax.axis_index("dp") % 2) * capacity, capacity)
    part = out_ref.shape[1]
    for slot, block in enumerate(packs):
        hid = block.shape[1] - part
        out_ref[slot * capacity : (slot + 1) * capacity] = block[pl.ds(start, capacity), hid:]


def mine(packs, part, capacity):
    return pl.pallas_call(
        functools.partial(mine_kernel, capacity),
        in_specs=[WHOLE] * len(packs),
        out_specs=WHOLE,
        out_shape=jax.ShapeDtypeStruct((len(packs) * capacity, part), bf16),
        compiler_params=pltpu.CompilerParams(vmem_limit_bytes=2 * 2**20),
        cost_estimate=work(1),
        name="own_columns",
    )(*packs)


def weight_kernel(capacity, peers, step, *rest):
    packs = rest[:peers]
    *parts, out_ref, rows_ref = rest[peers:]
    count = len(parts)
    rows = count * capacity

    @pl.when(pl.program_id(0) == 0)
    def _():
        for ahead, piece in enumerate(parts):
            block = lax.axis_index("seq") ^ ahead
            for slot in range(peers):
                start = pl.multiple_of(slot * rows + block * capacity, capacity)
                rows_ref[pl.ds(start, capacity), :] = piece[slot * capacity : (slot + 1) * capacity]

    lanes = pl.ds(pl.multiple_of(pl.program_id(0) * step, LANES), step)
    hidden = jnp.concatenate([block[:, lanes] for block in packs], axis=0)
    out_ref[...] = lax.dot_general(
        rows_ref[...], hidden, (((0,), (0,)), ((), ())), preferred_element_type=f32
    )


def weight_grad(packs, parts, part, capacity):
    peers = len(packs)
    rows = packs[0].shape[0]
    hid = packs[0].shape[1] - part
    step = hid // 2 if hid % (2 * LANES) == 0 else hid
    return pl.pallas_call(
        functools.partial(weight_kernel, capacity, peers, step),
        grid=(hid // step,),
        in_specs=[WHOLE] * (peers + len(parts)),
        out_specs=pl.BlockSpec((part, step), lambda c: (0, c)),
        out_shape=jax.ShapeDtypeStruct((part, hid), f32),
        scratch_shapes=[pltpu.VMEM((peers * rows, part), bf16)],
        compiler_params=pltpu.CompilerParams(vmem_limit_bytes=16 * 2**20),
        cost_estimate=work(3),
        name="weight_grad",
    )(*packs, *parts)


def routed_kernel(ids_ref, gate_ref, cot_ref, out_ref):
    out_ref[...] = slot_rows(ids_ref, gate_ref, cot_ref, out_ref.shape[0])


def routed_rows(ids, gate, cot, capacity):
    return pl.pallas_call(
        routed_kernel,
        out_shape=jax.ShapeDtypeStruct((capacity, cot.shape[1]), bf16),
        compiler_params=pltpu.CompilerParams(vmem_limit_bytes=8 * 2**20),
        cost_estimate=work(1),
        name="routed_rows",
    )(ids, gate, cot)


def from_ahead(value, axis, by):
    peers = lax.axis_size(axis)
    return lax.ppermute(value, axis, [(i, i - by) for i in range(by, peers)])


def across(value, axis, mask):
    return lax.ppermute(value, axis, [(i, i ^ mask) for i in range(lax.axis_size(axis))])


def on_device(
    cotangent,
    expert_ids,
    gate_probs,
    hidden_acts,
    step_input,
    step_proj,
    step_bias,
    decay_rate,
    input_coef,
    output_coef,
    grad_output,
    skip_weight,
):
    peers = lax.axis_size("dp")
    spans = lax.axis_size("seq")
    hid, rows = hidden_acts.shape
    features = cotangent.shape[2]
    capacity = rows // spans
    part = features // peers
    gathers = (
        peers * rows * 2 < features * 4
        and peers & (peers - 1) == 0
        and spans & (spans - 1) == 0
        and peers > 1
        and part % LANES == 0
        and hid % part == 0
        and 2 * capacity <= rows
    )
    masks = [0, *range(peers - 2, 0, -2)] if gathers else []
    expert = [expert_ids[0].T, gate_probs[0].T, cotangent[0], hidden_acts.T] if gathers else []
    step, later, message, *sent = state_pass(
        step_input[0],
        step_proj,
        step_bias,
        decay_rate,
        output_coef[0],
        grad_output[0],
        expert,
        masks,
        part,
        capacity,
    )
    messages = [from_ahead(message, "seq", by) for by in range(2, spans)]
    if gathers:
        near = [sent[0]] + [across(v, "dp", m) for v, m in zip(sent[1:], masks[1:])]
    local = local_pass(step, decay_rate, output_coef[0], input_coef[0], skip_weight, grad_output[0])

    if gathers:
        far, local, messages, message = lax.optimization_barrier((near[1:], local, messages, message))
        near = near[:1] + list(far)
        packs = near + [across(v, "dp", 1) for v in near]
        own = mine(packs, part, capacity)
        parts = [own] + [across(own, "seq", by) for by in range(1, spans)]
        grad_down = weight_grad(packs, parts, part, capacity)
    else:
        routed = routed_rows(expert_ids[0].T, gate_probs[0].T, cotangent[0], capacity)
        dense = lax.dot_general(
            lax.all_gather(routed, "seq", axis=0, tiled=True),
            hidden_acts,
            (((0,), (1,)), ((), ())),
            preferred_element_type=f32,
        )
        grad_down = lax.psum_scatter(dense, "dp", scatter_dimension=0, tiled=True)

    messages = [from_ahead(message, "seq", 1)] + list(messages)
    grad_x = carry_pass(local, step, later, decay_rate, input_coef[0], messages)[None]
    return (grad_down, grad_x)


def solution(mesh):
    return jax.shard_map(
        on_device,
        mesh=mesh,
        in_specs=(
            P("dp", "seq", None),
            P("dp", "seq", None),
            P("dp", "seq", None),
            P("seq", "dp"),
            P("dp", "seq", None),
            P(),
            P(),
            P(),
            P("dp", None, "seq"),
            P("dp", None, "seq"),
            P("dp", "seq", None),
            P(),
        ),
        out_specs=(P("dp", "seq"), P("dp", "seq", None)),
        check_vma=False,
    )
```
